32 devices in a mesh: illum: 8 (over z, x), slab: 2 (over core), cuts: 2 (over y).
Axes of the slice: x: 2, y: 2, z: 4, core: 2. Of those that a mesh axis runs over, the one named last changes fastest.
Arguments:
- phase_delay: float32 [4, 64, 1024], P('cuts', 'slab', 'illum'), may hold values from -1.5 to 1.5
- attenuation: float32 [4, 64, 1024], P('cuts', 'slab', 'illum'), may hold values from 0.02 to 0.3
- measured: float32 [8, 2, 64, 1024], P('illum', None, 'slab'), may hold values from -6 to 6
- angles: int32 [8, 2], P('illum'), may hold values from -16 to 16
Outputs:
- grad_phase: float32 [4, 64, 1024], P('cuts', 'slab', 'illum')
- grad_atten: float32 [4, 64, 1024], P('cuts', 'slab', 'illum')
The draws below stay inside these ranges and needn't reach their ends.
All inputs are finite; a program needn't handle non-finite values.
Results may differ from the reference program's by a relative error of at most 0.0001.
Values sent between devices are 32-bit elements; how exact they have to be, the bound alone decides.
A program may use at most 64 MiB of HBM per device.

```python
import math
import jax
import jax.numpy as jnp

NB = 1024
NA = 64
ILLUMS = 8
NZ = 4


def set_ends(result, key, least, top_value):
    longest = result.shape.index(max(result.shape))
    spots = []
    for shift in (0, 1):
        where = [jax.random.randint(jax.random.fold_in(key, axis), (), 0, length) for axis, length in enumerate(result.shape)]
        where[longest] = (where[longest] + shift) % result.shape[longest]
        spots.append(tuple(where))
    return result.at[spots[0]].set(least).at[spots[1]].set(top_value)


def level_of(rng, extent, shards, low, largest):
    gain, own = 1.0, jax.random.fold_in(rng, 6)
    for dim, blocks in shards:
        draws = jnp.exp(jax.random.uniform(jax.random.fold_in(own, dim), (blocks,), jnp.float32, low / len(shards), largest / len(shards)))
        gain = gain * jnp.repeat(draws, extent[dim] // blocks).reshape([-1 if axis == dim else 1 for axis in range(len(extent))])
    return gain


def normal_values(stream_key, shape, deviation, most, split=(), held_as=jnp.bfloat16):
    drawn = deviation * jax.random.normal(stream_key, shape, jnp.float32)
    if split:
        drawn = drawn * level_of(stream_key, shape, split, -0.22, 0.18)
    return jnp.clip(drawn, -most, most).astype(held_as)


def setup_inputs(seed: int = 0) -> dict:
    seeds = jax.random.split(jax.random.key(seed), 5)
    return {
        "phase_delay": jnp.clip(jax.random.uniform(seeds[0], (NZ, NA, NB), jnp.float32, -1.5, 1.5) * level_of(seeds[0], (NZ, NA, NB), ((0, 2), (1, 2), (2, 8)), -0.4, 0.0), -1.5, 1.5),
        "attenuation": jnp.clip(jnp.exp(math.log(0.3) - 2.7080503 * jax.random.uniform(seeds[1], (NZ, NA, NB), jnp.float32) ** level_of(seeds[1], (NZ, NA, NB), ((0, 2), (1, 2), (2, 8)), -0.2, 0.2)), 0.02, 0.3),
        "measured": normal_values(seeds[2], (ILLUMS, 2, NA, NB), 1.0, 6.0, ((0, 8), (2, 2)), jnp.float32),
        "angles": set_ends(jax.random.randint(seeds[3], (ILLUMS, 2), -16, 17), jax.random.fold_in(seeds[3], 1), -16, 16).astype(jnp.int32),
    }


step_coeff = 0.08
square_coeff = 0.0032


def laplace(values):
    padded = jnp.pad(values, ((0, 0), (0, 0), (1, 1), (1, 1)))
    return (padded[:, :, :-2, 1:-1] + padded[:, :, 2:, 1:-1] + padded[:, :, 1:-1, :-2]
            + padded[:, :, 1:-1, 2:] - 4.0 * values)


def diffract(fields, orient):
    laplace_one = laplace(fields)
    laplace_two = laplace(laplace_one)
    real_part = fields[:, 0] - orient * step_coeff * laplace_one[:, 1] - square_coeff * laplace_two[:, 0]
    imag_part = fields[:, 1] + orient * step_coeff * laplace_one[:, 0] - square_coeff * laplace_two[:, 1]
    return jnp.stack((real_part, imag_part), axis=1)


def incident_wave(angles, row_ids, total_rows, total_cols):
    column_ids = jnp.arange(total_cols, dtype=jnp.int32)
    row_turns = angles[:, 0].astype(jnp.int32)[:, None, None]
    col_turns = angles[:, 1].astype(jnp.int32)[:, None, None]
    fraction = (jnp.mod(row_turns * row_ids[None, :, None], total_rows).astype(jnp.float32) / total_rows
                + jnp.mod(col_turns * column_ids[None, None, :], total_cols).astype(jnp.float32) / total_cols)
    phase_angle = 2.0 * math.pi * fraction
    return jnp.stack((jnp.cos(phase_angle), jnp.sin(phase_angle)), axis=1)


def complex_times(pair, fields):
    trans_real, trans_imag = pair
    return jnp.stack((trans_real * fields[:, 0] - trans_imag * fields[:, 1],
                      trans_real * fields[:, 1] + trans_imag * fields[:, 0]), axis=1)


def conj_times(pair, fields):
    trans_real, trans_imag = pair
    return jnp.stack((trans_real * fields[:, 0] + trans_imag * fields[:, 1],
                      trans_real * fields[:, 1] - trans_imag * fields[:, 0]), axis=1)


def reference(phase_delay, attenuation, measured, angles):
    fields = incident_wave(angles, jnp.arange(NA, dtype=jnp.int32), NA, NB)
    transmit = []
    stored = []
    for layer_index in range(NZ):
        damping = jnp.exp(-attenuation[layer_index])
        pair = (damping * jnp.cos(phase_delay[layer_index]), damping * jnp.sin(phase_delay[layer_index]))
        transmit.append(pair)
        passed = complex_times(pair, fields)
        stored.append(passed)
        fields = diffract(passed, 1.0)
    adjoint = fields - measured
    phase_list = [None] * NZ
    atten_list = [None] * NZ
    for layer_index in reversed(range(NZ)):
        weighted = diffract(adjoint, -1.0)
        passed = stored[layer_index]
        phase_list[layer_index] = -jnp.sum(passed[:, 1] * weighted[:, 0] - passed[:, 0] * weighted[:, 1], axis=0)
        atten_list[layer_index] = -jnp.sum(passed[:, 0] * weighted[:, 0] + passed[:, 1] * weighted[:, 1], axis=0)
        adjoint = conj_times(transmit[layer_index], weighted)
    return jnp.stack(phase_list), jnp.stack(atten_list)
```

```python
import functools
import math

import jax
import jax.numpy as jnp
from jax import lax
from jax.experimental import pallas as pl
from jax.experimental.pallas import tpu as pltpu
from jax.sharding import PartitionSpec as P

MESH = pl.DeviceIdType.MESH
LANES = 128
PAD = 8

step_coeff = 0.08
square_coeff = 0.0032


def with_halo(cells, sides, width):
    for axis, dim in sides:
        count = lax.axis_size(axis)
        ends = count - 1
        head = lax.slice_in_dim(cells, 0, width, axis=dim)
        tail = lax.slice_in_dim(cells, cells.shape[dim] - width, cells.shape[dim], axis=dim)
        cells = jnp.concatenate(
            [
                lax.ppermute(tail, axis, [(i, (i + 1) % count) for i in range(ends)]),
                cells,
                lax.ppermute(head, axis, [((i + 1) % count, i) for i in range(ends)]),
            ],
            axis=dim,
        )
    return cells


def shifted(value, axis, steps):
    count = lax.axis_size(axis)
    leading, last = (max(0, -steps), min(count, count - steps))
    return lax.ppermute(value, axis, [(source, source + steps) for source in range(leading, last)])


def lap_rows(padded):
    center = padded[..., 1:-1, :]
    widths = ((0, 0),) * (center.ndim - 1) + ((1, 1),)
    sideways = jnp.pad(center, widths)
    return (
        padded[..., :-2, :]
        + padded[..., 2:, :]
        + sideways[..., :-2]
        + sideways[..., 2:]
        - 4.0 * center
    )


def incident_wave(angles, row_ids, total_rows, total_cols):
    column_ids = jnp.arange(total_cols, dtype=jnp.int32)
    row_turns = angles[:, 0][:, None, None]
    col_turns = angles[:, 1][:, None, None]
    fraction = (
        jnp.mod(row_turns * row_ids[None, :, None], total_rows).astype(jnp.float32) / total_rows
        + jnp.mod(col_turns * column_ids[None, None, :], total_cols).astype(jnp.float32)
        / total_cols
    )
    phase_angle = 2.0 * math.pi * fraction
    return jnp.stack((jnp.cos(phase_angle), jnp.sin(phase_angle)), axis=1)


def complex_times(pair, fields):
    trans_real, trans_imag = pair
    return jnp.stack(
        (
            trans_real * fields[:, 0] - trans_imag * fields[:, 1],
            trans_real * fields[:, 1] + trans_imag * fields[:, 0],
        ),
        axis=1,
    )


def conj_times(pair, fields):
    trans_real, trans_imag = pair
    return jnp.stack(
        (
            trans_real * fields[:, 0] + trans_imag * fields[:, 1],
            trans_real * fields[:, 1] - trans_imag * fields[:, 0],
        ),
        axis=1,
    )


def body(phase_delay, attenuation, measured, angles):
    n_cuts = lax.axis_size("cuts")
    cut_index = lax.axis_index("cuts")
    slab_index = lax.axis_index("slab")
    slab_rows = measured.shape[2]
    n_cols = measured.shape[3]
    total_rows = slab_rows * lax.axis_size("slab")
    row_start = slab_index * slab_rows
    local_phase, local_atten = (phase_delay, attenuation)
    slices_here = local_phase.shape[0]
    row_ids = row_start + jnp.arange(slab_rows, dtype=jnp.int32)
    start_fields = incident_wave(angles, row_ids, total_rows, n_cols)

    def stencil(fields):
        padded = with_halo(fields, (("slab", 2),), 2)
        wide_once = lap_rows(padded)
        wide_ids = row_start + jnp.arange(slab_rows + 2, dtype=jnp.int32) - 1
        inside = (wide_ids >= 0) & (wide_ids < total_rows)
        wide_once = jnp.where(inside[:, None], wide_once, 0.0)
        laplace_one = wide_once[:, :, 1:-1]
        laplace_two = lap_rows(wide_once)
        return (laplace_one, laplace_two)

    def diffract(fields, orient):
        laplace_one, laplace_two = stencil(fields)
        real_part = (
            fields[:, 0]
            - orient * step_coeff * laplace_one[:, 1]
            - square_coeff * laplace_two[:, 0]
        )
        imag_part = (
            fields[:, 1]
            + orient * step_coeff * laplace_one[:, 0]
            - square_coeff * laplace_two[:, 1]
        )
        return jnp.stack((real_part, imag_part), axis=1)

    whole_phase, whole_atten = (
        lax.all_gather(local_phase, "illum", axis=2, tiled=True),
        lax.all_gather(local_atten, "illum", axis=2, tiled=True),
    )
    transmit = []
    for layer_index in range(slices_here):
        damping = jnp.exp(-whole_atten[layer_index])
        transmit.append(
            (
                damping * jnp.cos(whole_phase[layer_index]),
                damping * jnp.sin(whole_phase[layer_index]),
            )
        )
    phase_list = [None] * slices_here
    atten_list = [None] * slices_here

    def record(layer_index, passed, weighted):
        phase_part = -jnp.sum(passed[:, 1] * weighted[:, 0] - passed[:, 0] * weighted[:, 1], axis=0)
        atten_part = -jnp.sum(passed[:, 0] * weighted[:, 0] + passed[:, 1] * weighted[:, 1], axis=0)
        phase_list[layer_index] = phase_part
        atten_list[layer_index] = atten_part

    entering = start_fields
    stored = []
    fields = start_fields
    for round_index in range(n_cuts):
        fields = entering
        stored = []
        for layer_index in range(slices_here):
            passed = complex_times(transmit[layer_index], fields)
            stored.append(passed)
            fields = diffract(passed, 1.0)
        if round_index < n_cuts - 1:
            received = shifted(fields, "cuts", 1)
            entering = jnp.where(cut_index == 0, start_fields, received)
    residual = fields - measured
    entering = residual
    for round_index in range(n_cuts):
        adjoint = entering
        last_round = round_index == n_cuts - 1
        for layer_index in reversed(range(slices_here)):
            weighted = diffract(adjoint, -1.0)
            if last_round:
                record(layer_index, stored[layer_index], weighted)
            adjoint = conj_times(transmit[layer_index], weighted)
        if not last_round:
            received = shifted(adjoint, "cuts", -1)
            entering = jnp.where(cut_index == n_cuts - 1, residual, received)
    grad_phase, grad_atten = (
        lax.psum_scatter(jnp.stack(phase_list), "illum", scatter_dimension=2, tiled=True),
        lax.psum_scatter(jnp.stack(atten_list), "illum", scatter_dimension=2, tiled=True),
    )
    return (grad_phase, grad_atten)


def suits(phase_delay, attenuation, measured, angles):
    illums, slabs, cuts = (lax.axis_size(name) for name in ("illum", "slab", "cuts"))
    depth, rows, width = phase_delay.shape
    halo = 4 * depth * cuts
    return (
        width == LANES
        and rows % 8 == 0
        and measured.shape[0] == 1
        and measured.shape[3] == illums * LANES
        and illums % (slabs * cuts) == 0
        and illums % cuts == 0
        and slabs > 1
        and illums // (slabs * cuts) <= 4
        and slabs * rows <= 128
        and LANES % (2 * depth) == 0
        and 2 * depth * 2 * halo <= LANES
    )


def sincos_turns(turns):
    quarter = jnp.round(4.0 * turns)
    angle = (turns - 0.25 * quarter) * (2.0 * math.pi)
    square = angle * angle
    sine = angle * (
        1.0 + square * (-1.0 / 6 + square * (1.0 / 120 + square * (-1.0 / 5040 + square / 362880)))
    )
    cosine = 1.0 + square * (
        -0.5 + square * (1.0 / 24 + square * (-1.0 / 720 + square / 40320))
    )
    place = quarter - 4.0 * jnp.floor(0.25 * quarter)
    odd = (place == 1.0) | (place == 3.0)
    first = jnp.where(odd, sine, cosine)
    second = jnp.where(odd, cosine, sine)
    cos_value = jnp.where((place == 1.0) | (place == 2.0), -first, first)
    sin_value = jnp.where(place >= 2.0, -second, second)
    return cos_value, sin_value


def fused_kernel(
    sizes,
    phase_ref,
    atten_ref,
    measured_ref,
    angles_ref,
    out_phase_ref,
    out_atten_ref,
    trans,
    trans_edge,
    edge_own,
    edges,
    message,
    arrived,
    angle_own,
    angle_in,
    fields,
    laps,
    parts,
    others,
    angle_send,
    angle_recv,
    trans_send,
    trans_recv,
    edge_send,
    edge_recv,
    message_send,
    message_recv,
    part_send,
    part_recv,
):
    illums, slabs, cuts, depth, rows = sizes
    members = slabs * cuts
    slots = illums // members
    turns = illums // cuts
    slices = depth * cuts
    total_rows = slabs * rows
    total_cols = illums * LANES
    planes = 2 * depth
    share = LANES // planes

    block = lax.axis_index("illum")
    slab = lax.axis_index("slab")
    cut = lax.axis_index("cuts")
    member = block % members
    to_slab, to_cut, slot = member % slabs, member // slabs, block // members
    offsets = [(ds, dc) for ds in range(slabs) for dc in range(cuts) if ds + dc > 0]
    everyone = [(s, c) for s in range(slabs) for c in range(cuts)]
    loops_back = (block % cuts == cut) & (to_slab == slab) & (to_cut == cut)

    barrier = pltpu.get_barrier_semaphore()

    def greet(device):
        pl.semaphore_signal(barrier, inc=1, device_id=device, device_id_type=MESH)

    for ds, dc in offsets:
        greet((block, (slab + ds) % slabs, (cut + dc) % cuts))
    for step in (-1, 1):

        @pl.when((block + step >= 0) & (block + step < illums))
        def _(step=step):
            for s, c in everyone:
                greet((block + step, s, c))

    for b in range(slots):
        for s in range(slabs):
            source = members * b + slabs * cut + slab

            @pl.when(jnp.logical_not((source == block) & (slab == s) & (cut == block % cuts)))
            def _(source=source, s=s):
                greet((source, s, block % cuts))

    lane = lax.broadcasted_iota(jnp.int32, (1, LANES), 1)

    packed = None
    for k in range(depth):
        damping = jnp.exp(-atten_ref[k])
        cosine, sine = sincos_turns(phase_ref[k] * (0.5 / math.pi))
        for part, value in ((0, damping * cosine), (1, damping * sine)):
            trans[cut, slab, k, part] = value
            q = 2 * k + part
            if q == 0:
                packed = value
            else:
                here = (lane >= share * q - share // 2) & (lane < share * q + share // 2)
                packed = jnp.where(here, pltpu.roll(value, share * q, 1), packed)
    edge_own[...] = packed
    angle_rows = lax.broadcasted_iota(jnp.int32, (8, LANES), 0)
    angle_own[...] = jnp.where(angle_rows < 4, angles_ref[0, 0], angles_ref[0, 1]).astype(
        jnp.float32
    )

    inside_low = (block > 0).astype(jnp.int32)
    inside_high = (block < illums - 1).astype(jnp.int32)
    pl.semaphore_wait(
        barrier,
        len(offsets) + members * (inside_low + inside_high) + turns - loops_back.astype(jnp.int32),
    )

    def angle_copy(b, t, device):
        return pltpu.make_async_remote_copy(
            angle_own, angle_in.at[b], angle_send.at[t], angle_recv.at[b], device, MESH
        )

    def trans_copy(c, s, ds, dc, device):
        return pltpu.make_async_remote_copy(
            trans.at[c, s],
            trans.at[c, s],
            trans_send.at[ds, dc],
            trans_recv.at[ds, dc],
            device,
            MESH,
        )

    def edge_copy(side, c, s, to_s, to_c, device):
        return pltpu.make_async_remote_copy(
            edge_own,
            edges.at[side, c, s],
            edge_send.at[side, to_c, to_s],
            edge_recv.at[side, c, s],
            device,
            MESH,
        )

    def message_copy(b, s, t, device):
        return pltpu.make_async_remote_copy(
            message.at[t],
            arrived.at[b, s],
            message_send.at[t],
            message_recv.at[b, s],
            device,
            MESH,
        )

    sends_angles = slab == (to_slab + 1) % slabs

    @pl.when(sends_angles)
    def _():
        for t in range(turns):
            angle_copy(slot, t, (cuts * t + cut, to_slab, to_cut)).start()

    for ds, dc in offsets:
        trans_copy(cut, slab, ds, dc, (block, (slab + ds) % slabs, (cut + dc) % cuts)).start()
    for side, step in ((0, 1), (1, -1)):

        @pl.when((block + step >= 0) & (block + step < illums))
        def _(side=side, step=step):
            for s, c in everyone:
                edge_copy(side, cut, slab, s, c, (block + step, s, c)).start()

        @pl.when(jnp.logical_not((block - step >= 0) & (block - step < illums)))
        def _(side=side):
            edges[side] = jnp.zeros(edges.shape[1:], jnp.float32)

    for t in range(turns):
        target = cuts * t + cut
        before, after = jnp.maximum(target - 1, 0), jnp.minimum(target + 1, illums - 1)

        def tile(part, at):
            return measured_ref[0, part, :, pl.ds(pl.multiple_of(at * LANES, LANES), LANES)]

        rims = []
        for part in range(2):
            message[t, part] = tile(part, target)
            rims.append(jnp.where(lane < LANES // 2, tile(part, after), tile(part, before)))
        middle = (lane >= LANES // 4) & (lane < 3 * LANES // 4)
        message[t, 2] = jnp.where(middle, pltpu.roll(rims[1], LANES // 2, 1), rims[0])
        to_self = (target == block) & loops_back

        @pl.when(jnp.logical_not(to_self))
        def _(t=t, target=target):
            message_copy(slot, slab, t, (target, to_slab, to_cut)).start()

        @pl.when(to_self)
        def _(t=t):
            arrived[slot, slab] = message[t]

    for ref in (fields, laps):
        zero = jnp.zeros(ref.shape[:-2] + (PAD, LANES), jnp.float32)
        ref[..., 0:PAD, :] = zero
        ref[..., PAD + total_rows : 2 * PAD + total_rows, :] = zero

    lead = lane < LANES // 2
    outside = (lead & (block == illums - 1)) | (jnp.logical_not(lead) & (block == 0))
    keep = jnp.where(outside, 0.0, 1.0)
    first_lane, last_lane = lane == 0, lane == LANES - 1

    def laplace(ref, b, slab_id):
        top = PAD + slab_id * rows
        center, vertical, left, right = [], [], [], []
        for tile_id in range(2):
            value = ref[tile_id, b, :, top : top + rows, :]
            center.append(value)
            vertical.append(
                ref[tile_id, b, :, top - 1 : top + rows - 1, :]
                + ref[tile_id, b, :, top + 1 : top + rows + 1, :]
            )
            left.append(pltpu.roll(value, 1, 2))
            right.append(pltpu.roll(value, LANES - 1, 2))
        found = []
        for tile_id in range(2):
            sideways = jnp.where(first_lane, left[1 - tile_id], left[tile_id]) + jnp.where(
                last_lane, right[1 - tile_id], right[tile_id]
            )
            found.append(vertical[tile_id] + sideways - 4.0 * center[tile_id])
        return center, found

    def laplace_pass(ref):
        for b in range(slots):
            for slab_id in range(slabs):
                top = PAD + slab_id * rows
                _, found = laplace(ref, b, slab_id)
                laps[0, b, :, top : top + rows, :] = found[0]
                laps[1, b, :, top : top + rows, :] = found[1] * keep

    def diffracted(ref, b, slab_id, orient):
        top = PAD + slab_id * rows
        once, twice = laplace(laps, b, slab_id)
        result = []
        for tile_id in range(2):
            real = ref[tile_id, b, 0, top : top + rows, :]
            imag = ref[tile_id, b, 1, top : top + rows, :]
            result.append(
                (
                    real
                    - orient * step_coeff * once[tile_id][1]
                    - square_coeff * twice[tile_id][0],
                    imag
                    + orient * step_coeff * once[tile_id][0]
                    - square_coeff * twice[tile_id][1],
                )
            )
        return result

    def pair(tile_id, layer, slab_id):
        ref = trans if tile_id == 0 else trans_edge
        return (
            ref[layer // depth, slab_id, layer % depth, 0],
            ref[layer // depth, slab_id, layer % depth, 1],
        )

    def store(ref, tile_id, b, slab_id, real, imag):
        top = PAD + slab_id * rows
        ref[tile_id, b, 0, top : top + rows, :] = real
        ref[tile_id, b, 1, top : top + rows, :] = imag

    def pass_on(layer, tile_id, b, slab_id, real, imag):
        trans_real, trans_imag = pair(tile_id, layer, slab_id)
        store(
            fields.at[layer],
            tile_id,
            b,
            slab_id,
            trans_real * real - trans_imag * imag,
            trans_real * imag + trans_imag * real,
        )

    for b in range(slots):
        angle_copy(
            b, 0, (members * b + slabs * cut + slab, (slab + 1) % slabs, block % cuts)
        ).wait_recv()
    starts = {}
    columns = (
        (block * LANES + lane),
        jnp.where(lead, (block + 1) * LANES + lane, (block - 1) * LANES + lane),
    )
    for b in range(slots):
        row_turns = angle_in[b, 0:1, :]
        col_turns = angle_in[b, 4:5, :]
        for tile_id in range(2):
            col_part = col_turns * columns[tile_id].astype(jnp.float32) * (1.0 / total_cols)
            for slab_id in range(slabs):
                row_ids = lax.broadcasted_iota(jnp.int32, (rows, LANES), 0) + slab_id * rows
                row_part = row_turns * row_ids.astype(jnp.float32) * (1.0 / total_rows)
                whole = (col_part - jnp.floor(col_part)) + (row_part - jnp.floor(row_part))
                real, imag = sincos_turns(whole)
                store(fields.at[0], tile_id, b, slab_id, real, imag)

    for ds, dc in offsets:
        trans_copy(
            (cut + cuts - dc) % cuts,
            (slab + slabs - ds) % slabs,
            ds,
            dc,
            (block, (slab + slabs - ds) % slabs, (cut + cuts - dc) % cuts),
        ).wait_recv()
    for side, step in ((0, -1), (1, 1)):

        @pl.when((block + step >= 0) & (block + step < illums))
        def _(side=side, step=step):
            for s, c in everyone:
                edge_copy(side, c, s, s, c, (block + step, s, c)).wait_recv()

    from_right = lane % share < share // 2
    for s, c in everyone:
        both = jnp.where(from_right, edges[1, c, s], edges[0, c, s])
        for q in range(planes):
            trans_edge[c, s, q // 2, q % 2] = (
                both if q == 0 else pltpu.roll(both, LANES - share * q, 1)
            )

    for b in range(slots):
        for tile_id in range(2):
            for slab_id in range(slabs):
                top = PAD + slab_id * rows
                real = fields[0, tile_id, b, 0, top : top + rows, :]
                imag = fields[0, tile_id, b, 1, top : top + rows, :]
                pass_on(0, tile_id, b, slab_id, real, imag)

    adjoint = fields.at[slices]
    for layer in range(slices):
        laplace_pass(fields.at[layer])
        if layer == slices - 1:
            for b in range(slots):
                source = members * b + slabs * cut + slab
                for s in range(slabs):

                    @pl.when(
                        jnp.logical_not((source == block) & (slab == s) & (cut == block % cuts))
                    )
                    def _(b=b, s=s, source=source):
                        message_copy(b, s, 0, (source, s, block % cuts)).wait_recv()

        for b in range(slots):
            for slab_id in range(slabs):
                result = diffracted(fields.at[layer], b, slab_id, 1.0)
                if layer < slices - 1:
                    for tile_id in range(2):
                        pass_on(layer + 1, tile_id, b, slab_id, *result[tile_id])
                else:
                    rim = arrived[b, slab_id, 2]
                    store(
                        adjoint,
                        0,
                        b,
                        slab_id,
                        result[0][0] - arrived[b, slab_id, 0],
                        result[0][1] - arrived[b, slab_id, 1],
                    )
                    store(
                        adjoint,
                        1,
                        b,
                        slab_id,
                        (result[1][0] - rim) * keep,
                        (result[1][1] - pltpu.roll(rim, LANES // 2, 1)) * keep,
                    )

    def part_copy(layer, slab_id):
        to = layer // depth
        ds = (slab_id + slabs - slab) % slabs
        dc = (to + cuts - cut) % cuts
        return pltpu.make_async_remote_copy(
            parts.at[layer, slab_id],
            others.at[dc, ds, layer % depth],
            part_send.at[layer, slab_id],
            part_recv.at[dc, ds, layer % depth],
            (block, slab_id, to),
            MESH,
        )

    def not_own(layer, slab_id):
        return jnp.logical_not((slab == slab_id) & (cut == layer // depth))

    for layer in reversed(range(slices)):
        laplace_pass(adjoint)
        for slab_id in range(slabs):
            top = PAD + slab_id * rows
            phase_sum, atten_sum = None, None
            for b in range(slots):
                result = diffracted(adjoint, b, slab_id, -1.0)
                real, imag = result[0]
                passed_real = fields[layer, 0, b, 0, top : top + rows, :]
                passed_imag = fields[layer, 0, b, 1, top : top + rows, :]
                phase_part = passed_real * imag - passed_imag * real
                atten_part = -(passed_real * real + passed_imag * imag)
                phase_sum = phase_part if b == 0 else phase_sum + phase_part
                atten_sum = atten_part if b == 0 else atten_sum + atten_part
                if layer > 0:
                    for tile_id in range(2):
                        real, imag = result[tile_id]
                        trans_real, trans_imag = pair(tile_id, layer, slab_id)
                        store(
                            adjoint,
                            tile_id,
                            b,
                            slab_id,
                            trans_real * real + trans_imag * imag,
                            trans_real * imag - trans_imag * real,
                        )
            parts[layer, slab_id, 0] = phase_sum
            parts[layer, slab_id, 1] = atten_sum

            @pl.when(not_own(layer, slab_id))
            def _(layer=layer, slab_id=slab_id):
                part_copy(layer, slab_id).start()

    for k in reversed(range(depth)):
        phase_sum = parts[cut * depth + k, slab, 0]
        atten_sum = parts[cut * depth + k, slab, 1]
        for ds, dc in offsets:
            pltpu.make_async_remote_copy(
                parts.at[k, 0],
                others.at[dc, ds, k],
                part_send.at[k, 0],
                part_recv.at[dc, ds, k],
                (block, (slab + slabs - ds) % slabs, (cut + cuts - dc) % cuts),
                MESH,
            ).wait_recv()
            phase_sum = phase_sum + others[dc, ds, k, 0]
            atten_sum = atten_sum + others[dc, ds, k, 1]
        out_phase_ref[k] = phase_sum
        out_atten_ref[k] = atten_sum

    @pl.when(sends_angles)
    def _():
        for t in range(turns):
            angle_copy(slot, t, (cuts * t + cut, to_slab, to_cut)).wait_send()

    for ds, dc in offsets:
        trans_copy(cut, slab, ds, dc, (block, (slab + ds) % slabs, (cut + dc) % cuts)).wait_send()
    for side, step in ((0, 1), (1, -1)):

        @pl.when((block + step >= 0) & (block + step < illums))
        def _(side=side, step=step):
            for s, c in everyone:
                edge_copy(side, cut, slab, s, c, (block + step, s, c)).wait_send()

    for t in range(turns):
        target = cuts * t + cut

        @pl.when(jnp.logical_not((target == block) & loops_back))
        def _(t=t, target=target):
            message_copy(slot, slab, t, (target, to_slab, to_cut)).wait_send()

    for layer in range(slices):
        for slab_id in range(slabs):

            @pl.when(not_own(layer, slab_id))
            def _(layer=layer, slab_id=slab_id):
                part_copy(layer, slab_id).wait_send()


def fused(phase_delay, attenuation, measured, angles):
    illums, slabs, cuts = (lax.axis_size(name) for name in ("illum", "slab", "cuts"))
    depth, rows, _ = phase_delay.shape
    slots, turns, slices = illums // (slabs * cuts), illums // cuts, depth * cuts
    tall = slabs * rows + 2 * PAD

    def real(*shape):
        return pltpu.VMEM(shape, jnp.float32)

    dma = pltpu.SemaphoreType.DMA
    vmem = pl.BlockSpec(memory_space=pltpu.VMEM)
    return pl.pallas_call(
        functools.partial(fused_kernel, (illums, slabs, cuts, depth, rows)),
        out_shape=(
            jax.ShapeDtypeStruct(phase_delay.shape, jnp.float32),
            jax.ShapeDtypeStruct(phase_delay.shape, jnp.float32),
        ),
        in_specs=[vmem, vmem, vmem, pl.BlockSpec(memory_space=pltpu.SMEM)],
        out_specs=(vmem, vmem),
        scratch_shapes=[
            real(cuts, slabs, depth, 2, rows, LANES),
            real(cuts, slabs, depth, 2, rows, LANES),
            real(rows, LANES),
            real(2, cuts, slabs, rows, LANES),
            real(turns, 3, rows, LANES),
            real(slots, slabs, 3, rows, LANES),
            real(8, LANES),
            real(slots, 8, LANES),
            real(slices + 1, 2, slots, 2, tall, LANES),
            real(2, slots, 2, tall, LANES),
            real(slices, slabs, 2, rows, LANES),
            real(cuts, slabs, depth, 2, rows, LANES),
            dma((turns,)),
            dma((slots,)),
            dma((slabs, cuts)),
            dma((slabs, cuts)),
            dma((2, cuts, slabs)),
            dma((2, cuts, slabs)),
            dma((turns,)),
            dma((slots, slabs)),
            dma((slices, slabs)),
            dma((cuts, slabs, depth)),
        ],
        compiler_params=pltpu.CompilerParams(
            collective_id=0, has_side_effects=True, vmem_limit_bytes=32 * 1024 * 1024
        ),
    )(phase_delay, attenuation, measured, angles)


def solution(mesh):
    placed = (
        P("cuts", "slab", "illum"),
        P("cuts", "slab", "illum"),
        P("illum", None, "slab", None),
        P("illum", None),
    )

    def chosen(*blocks):
        return (fused if suits(*blocks) else body)(*blocks)

    return jax.shard_map(
        chosen,
        mesh=mesh,
        in_specs=placed,
        out_specs=(P("cuts", "slab", "illum"), P("cuts", "slab", "illum")),
        check_vma=False,
    )
```

```python
import functools
import math

import jax
import jax.numpy as jnp
from jax import lax
from jax.experimental import pallas as pl
from jax.experimental.pallas import tpu as pltpu
from jax.sharding import PartitionSpec as P

MESH = pl.DeviceIdType.MESH
LANES = 128
PAD = 8

step_coeff = 0.08
square_coeff = 0.0032


def with_halo(cells, sides, width):
    for axis, dim in sides:
        count = lax.axis_size(axis)
        ends = count - 1
        head = lax.slice_in_dim(cells, 0, width, axis=dim)
        tail = lax.slice_in_dim(cells, cells.shape[dim] - width, cells.shape[dim], axis=dim)
        cells = jnp.concatenate(
            [
                lax.ppermute(tail, axis, [(i, (i + 1) % count) for i in range(ends)]),
                cells,
                lax.ppermute(head, axis, [((i + 1) % count, i) for i in range(ends)]),
            ],
            axis=dim,
        )
    return cells


def shifted(value, axis, steps):
    count = lax.axis_size(axis)
    leading, last = (max(0, -steps), min(count, count - steps))
    return lax.ppermute(value, axis, [(source, source + steps) for source in range(leading, last)])


def lap_rows(padded):
    center = padded[..., 1:-1, :]
    widths = ((0, 0),) * (center.ndim - 1) + ((1, 1),)
    sideways = jnp.pad(center, widths)
    return (
        padded[..., :-2, :]
        + padded[..., 2:, :]
        + sideways[..., :-2]
        + sideways[..., 2:]
        - 4.0 * center
    )


def incident_wave(angles, row_ids, total_rows, total_cols):
    column_ids = jnp.arange(total_cols, dtype=jnp.int32)
    row_turns = angles[:, 0][:, None, None]
    col_turns = angles[:, 1][:, None, None]
    fraction = (
        jnp.mod(row_turns * row_ids[None, :, None], total_rows).astype(jnp.float32) / total_rows
        + jnp.mod(col_turns * column_ids[None, None, :], total_cols).astype(jnp.float32)
        / total_cols
    )
    phase_angle = 2.0 * math.pi * fraction
    return jnp.stack((jnp.cos(phase_angle), jnp.sin(phase_angle)), axis=1)


def complex_times(pair, fields):
    trans_real, trans_imag = pair
    return jnp.stack(
        (
            trans_real * fields[:, 0] - trans_imag * fields[:, 1],
            trans_real * fields[:, 1] + trans_imag * fields[:, 0],
        ),
        axis=1,
    )


def conj_times(pair, fields):
    trans_real, trans_imag = pair
    return jnp.stack(
        (
            trans_real * fields[:, 0] + trans_imag * fields[:, 1],
            trans_real * fields[:, 1] - trans_imag * fields[:, 0],
        ),
        axis=1,
    )


def body(phase_delay, attenuation, measured, angles):
    n_cuts = lax.axis_size("cuts")
    cut_index = lax.axis_index("cuts")
    slab_index = lax.axis_index("slab")
    slab_rows = measured.shape[2]
    n_cols = measured.shape[3]
    total_rows = slab_rows * lax.axis_size("slab")
    row_start = slab_index * slab_rows
    local_phase, local_atten = (phase_delay, attenuation)
    slices_here = local_phase.shape[0]
    row_ids = row_start + jnp.arange(slab_rows, dtype=jnp.int32)
    start_fields = incident_wave(angles, row_ids, total_rows, n_cols)

    def stencil(fields):
        padded = with_halo(fields, (("slab", 2),), 2)
        wide_once = lap_rows(padded)
        wide_ids = row_start + jnp.arange(slab_rows + 2, dtype=jnp.int32) - 1
        inside = (wide_ids >= 0) & (wide_ids < total_rows)
        wide_once = jnp.where(inside[:, None], wide_once, 0.0)
        laplace_one = wide_once[:, :, 1:-1]
        laplace_two = lap_rows(wide_once)
        return (laplace_one, laplace_two)

    def diffract(fields, orient):
        laplace_one, laplace_two = stencil(fields)
        real_part = (
            fields[:, 0]
            - orient * step_coeff * laplace_one[:, 1]
            - square_coeff * laplace_two[:, 0]
        )
        imag_part = (
            fields[:, 1]
            + orient * step_coeff * laplace_one[:, 0]
            - square_coeff * laplace_two[:, 1]
        )
        return jnp.stack((real_part, imag_part), axis=1)

    whole_phase, whole_atten = (
        lax.all_gather(local_phase, "illum", axis=2, tiled=True),
        lax.all_gather(local_atten, "illum", axis=2, tiled=True),
    )
    transmit = []
    for layer_index in range(slices_here):
        damping = jnp.exp(-whole_atten[layer_index])
        transmit.append(
            (
                damping * jnp.cos(whole_phase[layer_index]),
                damping * jnp.sin(whole_phase[layer_index]),
            )
        )
    phase_list = [None] * slices_here
    atten_list = [None] * slices_here

    def record(layer_index, passed, weighted):
        phase_part = -jnp.sum(passed[:, 1] * weighted[:, 0] - passed[:, 0] * weighted[:, 1], axis=0)
        atten_part = -jnp.sum(passed[:, 0] * weighted[:, 0] + passed[:, 1] * weighted[:, 1], axis=0)
        phase_list[layer_index] = phase_part
        atten_list[layer_index] = atten_part

    entering = start_fields
    stored = []
    fields = start_fields
    for round_index in range(n_cuts):
        fields = entering
        stored = []
        for layer_index in range(slices_here):
            passed = complex_times(transmit[layer_index], fields)
            stored.append(passed)
            fields = diffract(passed, 1.0)
        if round_index < n_cuts - 1:
            received = shifted(fields, "cuts", 1)
            entering = jnp.where(cut_index == 0, start_fields, received)
    residual = fields - measured
    entering = residual
    for round_index in range(n_cuts):
        adjoint = entering
        last_round = round_index == n_cuts - 1
        for layer_index in reversed(range(slices_here)):
            weighted = diffract(adjoint, -1.0)
            if last_round:
                record(layer_index, stored[layer_index], weighted)
            adjoint = conj_times(transmit[layer_index], weighted)
        if not last_round:
            received = shifted(adjoint, "cuts", -1)
            entering = jnp.where(cut_index == n_cuts - 1, residual, received)
    grad_phase, grad_atten = (
        lax.psum_scatter(jnp.stack(phase_list), "illum", scatter_dimension=2, tiled=True),
        lax.psum_scatter(jnp.stack(atten_list), "illum", scatter_dimension=2, tiled=True),
    )
    return (grad_phase, grad_atten)


def suits(phase_delay, attenuation, measured, angles):
    illums, slabs, cuts = (lax.axis_size(name) for name in ("illum", "slab", "cuts"))
    depth, rows, width = phase_delay.shape
    halo = 4 * depth * cuts
    return (
        width == LANES
        and rows % 8 == 0
        and measured.shape[0] == 1
        and measured.shape[3] == illums * LANES
        and illums % (slabs * cuts) == 0
        and illums % (2 * cuts) == 0
        and rows % 32 == 0
        and LANES % (8 * depth * cuts) == 0
        and slabs > 1
        and illums // (slabs * cuts) <= 4
        and slabs * rows <= 128
        and LANES % (2 * depth) == 0
        and 2 * depth * 2 * halo <= LANES
    )


def sincos_turns(turns):
    quarter = jnp.round(4.0 * turns)
    angle = (turns - 0.25 * quarter) * (2.0 * math.pi)
    square = angle * angle
    sine = angle * (
        1.0 + square * (-1.0 / 6 + square * (1.0 / 120 + square * (-1.0 / 5040 + square / 362880)))
    )
    cosine = 1.0 + square * (
        -0.5 + square * (1.0 / 24 + square * (-1.0 / 720 + square / 40320))
    )
    place = quarter - 4.0 * jnp.floor(0.25 * quarter)
    odd = (place == 1.0) | (place == 3.0)
    first = jnp.where(odd, sine, cosine)
    second = jnp.where(odd, cosine, sine)
    cos_value = jnp.where((place == 1.0) | (place == 2.0), -first, first)
    sin_value = jnp.where(place >= 2.0, -second, second)
    return cos_value, sin_value


def fused_kernel(
    sizes,
    phase_hbm,
    atten_hbm,
    measured_hbm,
    angles_hbm,
    out_phase_ref,
    out_atten_ref,
    trans,
    trans_edge,
    edge_own,
    edges,
    message,
    arrived,
    angle_own,
    angle_in,
    fields,
    laps,
    parts,
    others,
    phase_ref,
    atten_ref,
    measured_ref,
    angles_ref,
    load_sem,
    angle_send,
    angle_recv,
    trans_send,
    trans_recv,
    edge_send,
    edge_recv,
    message_send,
    message_recv,
    part_send,
    part_recv,
):
    illums, slabs, cuts, depth, rows = sizes
    members = slabs * cuts
    slots = illums // members
    reach = 2 * depth * cuts
    bands = LANES // (4 * reach)
    band = rows // bands
    turns = illums // cuts
    slices = depth * cuts
    total_rows = slabs * rows
    total_cols = illums * LANES
    planes = 2 * depth
    share = LANES // planes

    block = lax.axis_index("illum")
    slab = lax.axis_index("slab")
    cut = lax.axis_index("cuts")
    own_pair, own_side = block // 2, block % 2
    entry = own_side + 2 * (own_pair // cuts)
    to_slab, slot = entry % slabs, entry // slabs
    phase_of_cut = (cut + cuts - own_pair % cuts) % cuts

    def target_of(t):
        return 2 * (cuts * (t // 2) + phase_of_cut) + t % 2

    def source_of(b):
        e = slab + slabs * b
        return 2 * (cuts * (e // 2) + phase_of_cut) + e % 2

    loads = [
        pltpu.make_async_copy(angles_hbm, angles_ref, load_sem.at[0]),
        pltpu.make_async_copy(phase_hbm, phase_ref, load_sem.at[1]),
        pltpu.make_async_copy(atten_hbm, atten_ref, load_sem.at[2]),
        pltpu.make_async_copy(measured_hbm, measured_ref, load_sem.at[3]),
    ]
    for load in loads:
        load.start()
    offsets = [(ds, dc) for ds in range(slabs) for dc in range(cuts) if ds + dc > 0]
    everyone = [(s, c) for s in range(slabs) for c in range(cuts)]
    loops_back = (phase_of_cut == own_pair % cuts) & (to_slab == slab)

    barrier = pltpu.get_barrier_semaphore()

    def greet(device):
        pl.semaphore_signal(barrier, inc=1, device_id=device, device_id_type=MESH)

    for ds, dc in offsets:
        greet((block, (slab + ds) % slabs, (cut + dc) % cuts))
    for step in (-1, 1):

        @pl.when((block + step >= 0) & (block + step < illums))
        def _(step=step):
            for s, c in everyone:
                greet((block + step, s, c))

    for b in range(slots):
        for s in range(slabs):
            source = source_of(b)

            @pl.when(jnp.logical_not((source == block) & (slab == s)))
            def _(source=source, s=s):
                greet((source, s, cut))

    lane = lax.broadcasted_iota(jnp.int32, (1, LANES), 1)

    loads[1].wait()
    loads[2].wait()
    packed = None
    for k in range(depth):
        damping = jnp.exp(-atten_ref[k])
        cosine, sine = sincos_turns(phase_ref[k] * (0.5 / math.pi))
        for part, value in ((0, damping * cosine), (1, damping * sine)):
            trans[cut, slab, k, part] = value
            q = 2 * k + part
            if q == 0:
                packed = value
            else:
                here = (lane >= share * q - share // 2) & (lane < share * q + share // 2)
                packed = jnp.where(here, pltpu.roll(value, share * q, 1), packed)
    edge_own[...] = packed
    loads[0].wait()
    angle_rows = lax.broadcasted_iota(jnp.int32, (8, LANES), 0)
    angle_own[...] = jnp.where(angle_rows < 4, angles_ref[0, 0], angles_ref[0, 1]).astype(
        jnp.float32
    )

    loads[3].wait()
    for t in range(turns):
        target = target_of(t)
        before, after = jnp.maximum(target - 1, 0), jnp.minimum(target + 1, illums - 1)

        def tile(part, at):
            return measured_ref[0, part, :, pl.ds(pl.multiple_of(at * LANES, LANES), LANES)]

        rims = []
        for part in range(2):
            message[t, part * rows : (part + 1) * rows] = tile(part, target)
            rims.append(jnp.where(lane < LANES // 2, tile(part, after), tile(part, before)))
        second = (lane >= reach) & (lane < 3 * reach)
        rim = jnp.where(second, pltpu.roll(rims[1], 2 * reach, 1), rims[0])
        packed = rim[:band]
        for g in range(1, bands):
            here = ((lane + reach) // (4 * reach)) % bands == g
            moved = pltpu.roll(rim[g * band : (g + 1) * band], 4 * reach * g, 1)
            packed = jnp.where(here, moved, packed)
        message[t, 2 * rows :] = packed

    for ref in (fields, laps):
        zero = jnp.zeros(ref.shape[:-2] + (PAD, LANES), jnp.float32)
        ref[..., 0:PAD, :] = zero
        ref[..., PAD + total_rows : 2 * PAD + total_rows, :] = zero

    inside_low = (block > 0).astype(jnp.int32)
    inside_high = (block < illums - 1).astype(jnp.int32)
    pl.semaphore_wait(
        barrier,
        len(offsets) + members * (inside_low + inside_high) + turns - loops_back.astype(jnp.int32),
    )

    def angle_copy(b, t, device):
        return pltpu.make_async_remote_copy(
            angle_own, angle_in.at[b], angle_send.at[t], angle_recv.at[b], device, MESH
        )

    def trans_copy(c, s, ds, dc, device):
        return pltpu.make_async_remote_copy(
            trans.at[c, s],
            trans.at[c, s],
            trans_send.at[ds, dc],
            trans_recv.at[ds, dc],
            device,
            MESH,
        )

    def edge_copy(side, c, s, to_s, to_c, device):
        return pltpu.make_async_remote_copy(
            edge_own,
            edges.at[side, c, s],
            edge_send.at[side, to_c, to_s],
            edge_recv.at[side, c, s],
            device,
            MESH,
        )

    def message_copy(b, s, t, device):
        return pltpu.make_async_remote_copy(
            message.at[t],
            arrived.at[b, s],
            message_send.at[t],
            message_recv.at[b, s],
            device,
            MESH,
        )

    sends_angles = slab == (to_slab + 1) % slabs

    @pl.when(sends_angles)
    def _():
        for t in range(turns):
            angle_copy(slot, t, (target_of(t), to_slab, cut)).start()

    for ds, dc in offsets:
        trans_copy(cut, slab, ds, dc, (block, (slab + ds) % slabs, (cut + dc) % cuts)).start()
    for side, step in ((0, 1), (1, -1)):

        @pl.when((block + step >= 0) & (block + step < illums))
        def _(side=side, step=step):
            for s, c in everyone:
                edge_copy(side, cut, slab, s, c, (block + step, s, c)).start()

        @pl.when(jnp.logical_not((block - step >= 0) & (block - step < illums)))
        def _(side=side):
            edges[side] = jnp.zeros(edges.shape[1:], jnp.float32)

    for t in range(turns):
        target = target_of(t)
        to_self = (target == block) & loops_back

        @pl.when(jnp.logical_not(to_self))
        def _(t=t, target=target):
            message_copy(slot, slab, t, (target, to_slab, cut)).start()

        @pl.when(to_self)
        def _(t=t):
            arrived[slot, slab] = message[t]

    lead = lane < LANES // 2
    outside = (lead & (block == illums - 1)) | (jnp.logical_not(lead) & (block == 0))
    keep = jnp.where(outside, 0.0, 1.0)
    first_lane, last_lane = lane == 0, lane == LANES - 1

    def laplace(ref, b, slab_id):
        top = PAD + slab_id * rows
        center, vertical, left, right = [], [], [], []
        for tile_id in range(2):
            value = ref[tile_id, b, :, top : top + rows, :]
            center.append(value)
            vertical.append(
                ref[tile_id, b, :, top - 1 : top + rows - 1, :]
                + ref[tile_id, b, :, top + 1 : top + rows + 1, :]
            )
            left.append(pltpu.roll(value, 1, 2))
            right.append(pltpu.roll(value, LANES - 1, 2))
        found = []
        for tile_id in range(2):
            sideways = jnp.where(first_lane, left[1 - tile_id], left[tile_id]) + jnp.where(
                last_lane, right[1 - tile_id], right[tile_id]
            )
            found.append(vertical[tile_id] + sideways - 4.0 * center[tile_id])
        return center, found

    def laplace_pass(ref):
        for b in range(slots):
            for slab_id in range(slabs):
                top = PAD + slab_id * rows
                _, found = laplace(ref, b, slab_id)
                laps[0, b, :, top : top + rows, :] = found[0]
                laps[1, b, :, top : top + rows, :] = found[1] * keep

    def diffracted(ref, b, slab_id, orient):
        top = PAD + slab_id * rows
        once, twice = laplace(laps, b, slab_id)
        result = []
        for tile_id in range(2):
            real = ref[tile_id, b, 0, top : top + rows, :]
            imag = ref[tile_id, b, 1, top : top + rows, :]
            result.append(
                (
                    real
                    - orient * step_coeff * once[tile_id][1]
                    - square_coeff * twice[tile_id][0],
                    imag
                    + orient * step_coeff * once[tile_id][0]
                    - square_coeff * twice[tile_id][1],
                )
            )
        return result

    def pair(tile_id, layer, slab_id):
        ref = trans if tile_id == 0 else trans_edge
        return (
            ref[layer // depth, slab_id, layer % depth, 0],
            ref[layer // depth, slab_id, layer % depth, 1],
        )

    def store(ref, tile_id, b, slab_id, real, imag):
        top = PAD + slab_id * rows
        ref[tile_id, b, 0, top : top + rows, :] = real
        ref[tile_id, b, 1, top : top + rows, :] = imag

    def pass_on(layer, tile_id, b, slab_id, real, imag):
        trans_real, trans_imag = pair(tile_id, layer, slab_id)
        store(
            fields.at[layer],
            tile_id,
            b,
            slab_id,
            trans_real * real - trans_imag * imag,
            trans_real * imag + trans_imag * real,
        )

    for b in range(slots):
        angle_copy(
            b, 0, (source_of(b), (slab + 1) % slabs, cut)
        ).wait_recv()
    starts = {}
    columns = (
        (block * LANES + lane),
        jnp.where(lead, (block + 1) * LANES + lane, (block - 1) * LANES + lane),
    )
    for b in range(slots):
        row_turns = angle_in[b, 0:1, :]
        col_turns = angle_in[b, 4:5, :]
        for tile_id in range(2):
            col_part = col_turns * columns[tile_id].astype(jnp.float32) * (1.0 / total_cols)
            for slab_id in range(slabs):
                row_ids = lax.broadcasted_iota(jnp.int32, (rows, LANES), 0) + slab_id * rows
                row_part = row_turns * row_ids.astype(jnp.float32) * (1.0 / total_rows)
                whole = (col_part - jnp.floor(col_part)) + (row_part - jnp.floor(row_part))
                real, imag = sincos_turns(whole)
                store(fields.at[0], tile_id, b, slab_id, real, imag)

    for ds, dc in offsets:
        trans_copy(
            (cut + cuts - dc) % cuts,
            (slab + slabs - ds) % slabs,
            ds,
            dc,
            (block, (slab + slabs - ds) % slabs, (cut + cuts - dc) % cuts),
        ).wait_recv()
    for side, step in ((0, -1), (1, 1)):

        @pl.when((block + step >= 0) & (block + step < illums))
        def _(side=side, step=step):
            for s, c in everyone:
                edge_copy(side, c, s, s, c, (block + step, s, c)).wait_recv()

    from_right = lane % share < share // 2
    for s, c in everyone:
        both = jnp.where(from_right, edges[1, c, s], edges[0, c, s])
        for q in range(planes):
            trans_edge[c, s, q // 2, q % 2] = (
                both if q == 0 else pltpu.roll(both, LANES - share * q, 1)
            )

    for b in range(slots):
        for tile_id in range(2):
            for slab_id in range(slabs):
                top = PAD + slab_id * rows
                real = fields[0, tile_id, b, 0, top : top + rows, :]
                imag = fields[0, tile_id, b, 1, top : top + rows, :]
                pass_on(0, tile_id, b, slab_id, real, imag)

    adjoint = fields.at[slices]
    for layer in range(slices):
        laplace_pass(fields.at[layer])
        if layer == slices - 1:
            for b in range(slots):
                source = source_of(b)
                for s in range(slabs):

                    @pl.when(jnp.logical_not((source == block) & (slab == s)))
                    def _(b=b, s=s, source=source):
                        message_copy(b, s, 0, (source, s, cut)).wait_recv()

        for b in range(slots):
            for slab_id in range(slabs):
                result = diffracted(fields.at[layer], b, slab_id, 1.0)
                if layer < slices - 1:
                    for tile_id in range(2):
                        pass_on(layer + 1, tile_id, b, slab_id, *result[tile_id])
                else:
                    banded = arrived[b, slab_id, 2 * rows :]
                    rim = jnp.concatenate(
                        [banded]
                        + [pltpu.roll(banded, LANES - 4 * reach * g, 1) for g in range(1, bands)],
                        axis=0,
                    )
                    store(
                        adjoint,
                        0,
                        b,
                        slab_id,
                        result[0][0] - arrived[b, slab_id, :rows],
                        result[0][1] - arrived[b, slab_id, rows : 2 * rows],
                    )
                    store(
                        adjoint,
                        1,
                        b,
                        slab_id,
                        (result[1][0] - rim) * keep,
                        (result[1][1] - pltpu.roll(rim, LANES - 2 * reach, 1)) * keep,
                    )

    def part_copy(layer, slab_id):
        to = layer // depth
        ds = (slab_id + slabs - slab) % slabs
        dc = (to + cuts - cut) % cuts
        return pltpu.make_async_remote_copy(
            parts.at[layer, slab_id],
            others.at[dc, ds, layer % depth],
            part_send.at[layer, slab_id],
            part_recv.at[dc, ds, layer % depth],
            (block, slab_id, to),
            MESH,
        )

    def not_own(layer, slab_id):
        return jnp.logical_not((slab == slab_id) & (cut == layer // depth))

    for layer in reversed(range(slices)):
        laplace_pass(adjoint)
        for slab_id in range(slabs):
            top = PAD + slab_id * rows
            phase_sum, atten_sum = None, None
            for b in range(slots):
                result = diffracted(adjoint, b, slab_id, -1.0)
                real, imag = result[0]
                passed_real = fields[layer, 0, b, 0, top : top + rows, :]
                passed_imag = fields[layer, 0, b, 1, top : top + rows, :]
                phase_part = passed_real * imag - passed_imag * real
                atten_part = -(passed_real * real + passed_imag * imag)
                phase_sum = phase_part if b == 0 else phase_sum + phase_part
                atten_sum = atten_part if b == 0 else atten_sum + atten_part
                if layer > 0:
                    for tile_id in range(2):
                        real, imag = result[tile_id]
                        trans_real, trans_imag = pair(tile_id, layer, slab_id)
                        store(
                            adjoint,
                            tile_id,
                            b,
                            slab_id,
                            trans_real * real + trans_imag * imag,
                            trans_real * imag - trans_imag * real,
                        )
            parts[layer, slab_id, 0] = phase_sum
            parts[layer, slab_id, 1] = atten_sum

            @pl.when(not_own(layer, slab_id))
            def _(layer=layer, slab_id=slab_id):
                part_copy(layer, slab_id).start()

    for k in reversed(range(depth)):
        phase_sum = parts[cut * depth + k, slab, 0]
        atten_sum = parts[cut * depth + k, slab, 1]
        for ds, dc in offsets:
            pltpu.make_async_remote_copy(
                parts.at[k, 0],
                others.at[dc, ds, k],
                part_send.at[k, 0],
                part_recv.at[dc, ds, k],
                (block, (slab + slabs - ds) % slabs, (cut + cuts - dc) % cuts),
                MESH,
            ).wait_recv()
            phase_sum = phase_sum + others[dc, ds, k, 0]
            atten_sum = atten_sum + others[dc, ds, k, 1]
        out_phase_ref[k] = phase_sum
        out_atten_ref[k] = atten_sum

    @pl.when(sends_angles)
    def _():
        for t in range(turns):
            angle_copy(slot, t, (target_of(t), to_slab, cut)).wait_send()

    for ds, dc in offsets:
        trans_copy(cut, slab, ds, dc, (block, (slab + ds) % slabs, (cut + dc) % cuts)).wait_send()
    for side, step in ((0, 1), (1, -1)):

        @pl.when((block + step >= 0) & (block + step < illums))
        def _(side=side, step=step):
            for s, c in everyone:
                edge_copy(side, cut, slab, s, c, (block + step, s, c)).wait_send()

    for t in range(turns):
        target = target_of(t)

        @pl.when(jnp.logical_not((target == block) & loops_back))
        def _(t=t, target=target):
            message_copy(slot, slab, t, (target, to_slab, cut)).wait_send()

    for layer in range(slices):
        for slab_id in range(slabs):

            @pl.when(not_own(layer, slab_id))
            def _(layer=layer, slab_id=slab_id):
                part_copy(layer, slab_id).wait_send()


def fused(phase_delay, attenuation, measured, angles):
    illums, slabs, cuts = (lax.axis_size(name) for name in ("illum", "slab", "cuts"))
    depth, rows, _ = phase_delay.shape
    slots, turns, slices = illums // (slabs * cuts), illums // cuts, depth * cuts
    tall_message = 2 * rows + rows * 8 * slices // LANES
    tall = slabs * rows + 2 * PAD

    def real(*shape):
        return pltpu.VMEM(shape, jnp.float32)

    dma = pltpu.SemaphoreType.DMA
    vmem = pl.BlockSpec(memory_space=pltpu.VMEM)
    return pl.pallas_call(
        functools.partial(fused_kernel, (illums, slabs, cuts, depth, rows)),
        out_shape=(
            jax.ShapeDtypeStruct(phase_delay.shape, jnp.float32),
            jax.ShapeDtypeStruct(phase_delay.shape, jnp.float32),
        ),
        in_specs=[pl.BlockSpec(memory_space=pltpu.HBM)] * 4,
        out_specs=(vmem, vmem),
        scratch_shapes=[
            real(cuts, slabs, depth, 2, rows, LANES),
            real(cuts, slabs, depth, 2, rows, LANES),
            real(rows, LANES),
            real(2, cuts, slabs, rows, LANES),
            real(turns, tall_message, LANES),
            real(slots, slabs, tall_message, LANES),
            real(8, LANES),
            real(slots, 8, LANES),
            real(slices + 1, 2, slots, 2, tall, LANES),
            real(2, slots, 2, tall, LANES),
            real(slices, slabs, 2, rows, LANES),
            real(cuts, slabs, depth, 2, rows, LANES),
            real(*phase_delay.shape),
            real(*phase_delay.shape),
            real(*measured.shape),
            pltpu.SMEM(angles.shape, jnp.int32),
            dma((4,)),
            dma((turns,)),
            dma((slots,)),
            dma((slabs, cuts)),
            dma((slabs, cuts)),
            dma((2, cuts, slabs)),
            dma((2, cuts, slabs)),
            dma((turns,)),
            dma((slots, slabs)),
            dma((slices, slabs)),
            dma((cuts, slabs, depth)),
        ],
        compiler_params=pltpu.CompilerParams(
            collective_id=0, has_side_effects=True, vmem_limit_bytes=56 * 1024 * 1024
        ),
    )(phase_delay, attenuation, measured, angles)


def solution(mesh):
    placed = (
        P("cuts", "slab", "illum"),
        P("cuts", "slab", "illum"),
        P("illum", None, "slab", None),
        P("illum", None),
    )

    def chosen(*blocks):
        return (fused if suits(*blocks) else body)(*blocks)

    return jax.shard_map(
        chosen,
        mesh=mesh,
        in_specs=placed,
        out_specs=(P("cuts", "slab", "illum"), P("cuts", "slab", "illum")),
        check_vma=False,
    )
```

```python
import functools
import math

import jax
import jax.numpy as jnp
from jax import lax
from jax.experimental import pallas as pl
from jax.experimental.pallas import tpu as pltpu
from jax.sharding import PartitionSpec as P

MESH = pl.DeviceIdType.MESH
LANES = 128
PAD = 8

step_coeff = 0.08
square_coeff = 0.0032


def with_halo(cells, sides, width):
    for axis, dim in sides:
        count = lax.axis_size(axis)
        ends = count - 1
        head = lax.slice_in_dim(cells, 0, width, axis=dim)
        tail = lax.slice_in_dim(cells, cells.shape[dim] - width, cells.shape[dim], axis=dim)
        cells = jnp.concatenate(
            [
                lax.ppermute(tail, axis, [(i, (i + 1) % count) for i in range(ends)]),
                cells,
                lax.ppermute(head, axis, [((i + 1) % count, i) for i in range(ends)]),
            ],
            axis=dim,
        )
    return cells


def shifted(value, axis, steps):
    count = lax.axis_size(axis)
    leading, last = (max(0, -steps), min(count, count - steps))
    return lax.ppermute(value, axis, [(source, source + steps) for source in range(leading, last)])


def lap_rows(padded):
    center = padded[..., 1:-1, :]
    widths = ((0, 0),) * (center.ndim - 1) + ((1, 1),)
    sideways = jnp.pad(center, widths)
    return (
        padded[..., :-2, :]
        + padded[..., 2:, :]
        + sideways[..., :-2]
        + sideways[..., 2:]
        - 4.0 * center
    )


def incident_wave(angles, row_ids, total_rows, total_cols):
    column_ids = jnp.arange(total_cols, dtype=jnp.int32)
    row_turns = angles[:, 0][:, None, None]
    col_turns = angles[:, 1][:, None, None]
    fraction = (
        jnp.mod(row_turns * row_ids[None, :, None], total_rows).astype(jnp.float32) / total_rows
        + jnp.mod(col_turns * column_ids[None, None, :], total_cols).astype(jnp.float32)
        / total_cols
    )
    phase_angle = 2.0 * math.pi * fraction
    return jnp.stack((jnp.cos(phase_angle), jnp.sin(phase_angle)), axis=1)


def complex_times(pair, fields):
    trans_real, trans_imag = pair
    return jnp.stack(
        (
            trans_real * fields[:, 0] - trans_imag * fields[:, 1],
            trans_real * fields[:, 1] + trans_imag * fields[:, 0],
        ),
        axis=1,
    )


def conj_times(pair, fields):
    trans_real, trans_imag = pair
    return jnp.stack(
        (
            trans_real * fields[:, 0] + trans_imag * fields[:, 1],
            trans_real * fields[:, 1] - trans_imag * fields[:, 0],
        ),
        axis=1,
    )


def body(phase_delay, attenuation, measured, angles):
    n_cuts = lax.axis_size("cuts")
    cut_index = lax.axis_index("cuts")
    slab_index = lax.axis_index("slab")
    slab_rows = measured.shape[2]
    n_cols = measured.shape[3]
    total_rows = slab_rows * lax.axis_size("slab")
    row_start = slab_index * slab_rows
    local_phase, local_atten = (phase_delay, attenuation)
    slices_here = local_phase.shape[0]
    row_ids = row_start + jnp.arange(slab_rows, dtype=jnp.int32)
    start_fields = incident_wave(angles, row_ids, total_rows, n_cols)

    def stencil(fields):
        padded = with_halo(fields, (("slab", 2),), 2)
        wide_once = lap_rows(padded)
        wide_ids = row_start + jnp.arange(slab_rows + 2, dtype=jnp.int32) - 1
        inside = (wide_ids >= 0) & (wide_ids < total_rows)
        wide_once = jnp.where(inside[:, None], wide_once, 0.0)
        laplace_one = wide_once[:, :, 1:-1]
        laplace_two = lap_rows(wide_once)
        return (laplace_one, laplace_two)

    def diffract(fields, orient):
        laplace_one, laplace_two = stencil(fields)
        real_part = (
            fields[:, 0]
            - orient * step_coeff * laplace_one[:, 1]
            - square_coeff * laplace_two[:, 0]
        )
        imag_part = (
            fields[:, 1]
            + orient * step_coeff * laplace_one[:, 0]
            - square_coeff * laplace_two[:, 1]
        )
        return jnp.stack((real_part, imag_part), axis=1)

    whole_phase, whole_atten = (
        lax.all_gather(local_phase, "illum", axis=2, tiled=True),
        lax.all_gather(local_atten, "illum", axis=2, tiled=True),
    )
    transmit = []
    for layer_index in range(slices_here):
        damping = jnp.exp(-whole_atten[layer_index])
        transmit.append(
            (
                damping * jnp.cos(whole_phase[layer_index]),
                damping * jnp.sin(whole_phase[layer_index]),
            )
        )
    phase_list = [None] * slices_here
    atten_list = [None] * slices_here

    def record(layer_index, passed, weighted):
        phase_part = -jnp.sum(passed[:, 1] * weighted[:, 0] - passed[:, 0] * weighted[:, 1], axis=0)
        atten_part = -jnp.sum(passed[:, 0] * weighted[:, 0] + passed[:, 1] * weighted[:, 1], axis=0)
        phase_list[layer_index] = phase_part
        atten_list[layer_index] = atten_part

    entering = start_fields
    stored = []
    fields = start_fields
    for round_index in range(n_cuts):
        fields = entering
        stored = []
        for layer_index in range(slices_here):
            passed = complex_times(transmit[layer_index], fields)
            stored.append(passed)
            fields = diffract(passed, 1.0)
        if round_index < n_cuts - 1:
            received = shifted(fields, "cuts", 1)
            entering = jnp.where(cut_index == 0, start_fields, received)
    residual = fields - measured
    entering = residual
    for round_index in range(n_cuts):
        adjoint = entering
        last_round = round_index == n_cuts - 1
        for layer_index in reversed(range(slices_here)):
            weighted = diffract(adjoint, -1.0)
            if last_round:
                record(layer_index, stored[layer_index], weighted)
            adjoint = conj_times(transmit[layer_index], weighted)
        if not last_round:
            received = shifted(adjoint, "cuts", -1)
            entering = jnp.where(cut_index == n_cuts - 1, residual, received)
    grad_phase, grad_atten = (
        lax.psum_scatter(jnp.stack(phase_list), "illum", scatter_dimension=2, tiled=True),
        lax.psum_scatter(jnp.stack(atten_list), "illum", scatter_dimension=2, tiled=True),
    )
    return (grad_phase, grad_atten)


def suits(phase_delay, attenuation, measured, angles):
    illums, slabs, cuts = (lax.axis_size(name) for name in ("illum", "slab", "cuts"))
    depth, rows, width = phase_delay.shape
    halo = 4 * depth * cuts
    return (
        width == LANES
        and rows % 8 == 0
        and measured.shape[0] == 1
        and measured.shape[3] == illums * LANES
        and illums % (slabs * cuts) == 0
        and illums % (2 * cuts) == 0
        and rows % 32 == 0
        and LANES % (8 * depth * cuts) == 0
        and slabs > 1
        and illums // (slabs * cuts) <= 4
        and slabs * rows <= 128
        and LANES % (2 * depth) == 0
        and 2 * depth * 2 * halo <= LANES
    )


def sincos_turns(turns):
    quarter = jnp.round(4.0 * turns)
    angle = (turns - 0.25 * quarter) * (2.0 * math.pi)
    square = angle * angle
    sine = angle * (
        1.0 + square * (-1.0 / 6 + square * (1.0 / 120 + square * (-1.0 / 5040 + square / 362880)))
    )
    cosine = 1.0 + square * (
        -0.5 + square * (1.0 / 24 + square * (-1.0 / 720 + square / 40320))
    )
    place = quarter - 4.0 * jnp.floor(0.25 * quarter)
    odd = (place == 1.0) | (place == 3.0)
    first = jnp.where(odd, sine, cosine)
    second = jnp.where(odd, cosine, sine)
    cos_value = jnp.where((place == 1.0) | (place == 2.0), -first, first)
    sin_value = jnp.where(place >= 2.0, -second, second)
    return cos_value, sin_value


def fused_kernel(
    sizes,
    phase_hbm,
    atten_hbm,
    measured_hbm,
    angles_hbm,
    out_phase_ref,
    out_atten_ref,
    trans,
    trans_edge,
    edge_own,
    edges,
    message,
    arrived,
    angle_own,
    angle_in,
    fields,
    laps,
    parts,
    others,
    phase_ref,
    atten_ref,
    measured_ref,
    angles_ref,
    load_sem,
    angle_send,
    angle_recv,
    trans_send,
    trans_recv,
    edge_send,
    edge_recv,
    message_send,
    message_recv,
    part_send,
    part_recv,
):
    illums, slabs, cuts, depth, rows = sizes
    members = slabs * cuts
    slots = illums // members
    reach = 2 * depth * cuts
    bands = LANES // (4 * reach)
    band = rows // bands
    turns = illums // cuts
    slices = depth * cuts
    total_rows = slabs * rows
    total_cols = illums * LANES
    planes = 2 * depth
    share = LANES // planes

    block = lax.axis_index("illum")
    slab = lax.axis_index("slab")
    cut = lax.axis_index("cuts")
    own_pair, own_side = block // 2, block % 2
    entry = own_side + 2 * (own_pair // cuts)
    to_slab, slot = entry % slabs, entry // slabs
    phase_of_cut = (cut + cuts - own_pair % cuts) % cuts

    def target_of(t):
        return 2 * (cuts * (t // 2) + phase_of_cut) + t % 2

    def source_of(b):
        e = slab + slabs * b
        return 2 * (cuts * (e // 2) + phase_of_cut) + e % 2

    loads = [
        pltpu.make_async_copy(angles_hbm, angles_ref, load_sem.at[0]),
        pltpu.make_async_copy(phase_hbm, phase_ref, load_sem.at[1]),
        pltpu.make_async_copy(atten_hbm, atten_ref, load_sem.at[2]),
        pltpu.make_async_copy(measured_hbm, measured_ref, load_sem.at[3]),
    ]
    for load in loads:
        load.start()
    offsets = [(ds, dc) for ds in range(slabs) for dc in range(cuts) if ds + dc > 0]
    everyone = [(s, c) for s in range(slabs) for c in range(cuts)]
    loops_back = (phase_of_cut == own_pair % cuts) & (to_slab == slab)

    barrier = pltpu.get_barrier_semaphore()

    def greet(device):
        pl.semaphore_signal(barrier, inc=1, device_id=device, device_id_type=MESH)

    for ds, dc in offsets:
        greet((block, (slab + ds) % slabs, (cut + dc) % cuts))
    for step in (-1, 1):

        @pl.when((block + step >= 0) & (block + step < illums))
        def _(step=step):
            for s, c in everyone:
                greet((block + step, s, c))

    for b in range(slots):
        for s in range(slabs):
            source = source_of(b)

            @pl.when(jnp.logical_not((source == block) & (slab == s)))
            def _(source=source, s=s):
                greet((source, s, cut))

    lane = lax.broadcasted_iota(jnp.int32, (1, LANES), 1)

    loads[1].wait()
    loads[2].wait()
    packed = None
    for k in range(depth):
        damping = jnp.exp(-atten_ref[k])
        cosine, sine = sincos_turns(phase_ref[k] * (0.5 / math.pi))
        for part, value in ((0, damping * cosine), (1, damping * sine)):
            trans[cut, slab, k, part] = value
            q = 2 * k + part
            if q == 0:
                packed = value
            else:
                here = (lane >= share * q - share // 2) & (lane < share * q + share // 2)
                packed = jnp.where(here, pltpu.roll(value, share * q, 1), packed)
    edge_own[...] = packed
    loads[0].wait()
    angle_rows = lax.broadcasted_iota(jnp.int32, (8, LANES), 0)
    angle_own[...] = jnp.where(angle_rows < 4, angles_ref[0, 0], angles_ref[0, 1]).astype(
        jnp.float32
    )

    loads[3].wait()
    for t in range(turns):
        target = target_of(t)
        before, after = jnp.maximum(target - 1, 0), jnp.minimum(target + 1, illums - 1)

        def tile(part, at):
            return measured_ref[0, part, :, pl.ds(pl.multiple_of(at * LANES, LANES), LANES)]

        rims = []
        for part in range(2):
            message[t, part * rows : (part + 1) * rows] = tile(part, target)
            rims.append(jnp.where(lane < LANES // 2, tile(part, after), tile(part, before)))
        second = (lane >= reach) & (lane < 3 * reach)
        rim = jnp.where(second, pltpu.roll(rims[1], 2 * reach, 1), rims[0])
        packed = rim[:band]
        for g in range(1, bands):
            here = ((lane + reach) // (4 * reach)) % bands == g
            moved = pltpu.roll(rim[g * band : (g + 1) * band], 4 * reach * g, 1)
            packed = jnp.where(here, moved, packed)
        message[t, 2 * rows :] = packed

    for ref in (fields, laps):
        zero = jnp.zeros(ref.shape[:-2] + (PAD, LANES), jnp.float32)
        ref[..., 0:PAD, :] = zero
        ref[..., PAD + total_rows : 2 * PAD + total_rows, :] = zero

    inside_low = (block > 0).astype(jnp.int32)
    inside_high = (block < illums - 1).astype(jnp.int32)
    pl.semaphore_wait(
        barrier,
        len(offsets) + members * (inside_low + inside_high) + turns - loops_back.astype(jnp.int32),
    )

    def angle_copy(b, t, device):
        return pltpu.make_async_remote_copy(
            angle_own, angle_in.at[b], angle_send.at[t], angle_recv.at[b], device, MESH
        )

    def trans_copy(c, s, ds, dc, device):
        return pltpu.make_async_remote_copy(
            trans.at[c, s],
            trans.at[c, s],
            trans_send.at[ds, dc],
            trans_recv.at[ds, dc],
            device,
            MESH,
        )

    def edge_copy(side, c, s, to_s, to_c, device):
        return pltpu.make_async_remote_copy(
            edge_own,
            edges.at[side, c, s],
            edge_send.at[side, to_c, to_s],
            edge_recv.at[side, c, s],
            device,
            MESH,
        )

    def message_copy(b, s, t, device):
        return pltpu.make_async_remote_copy(
            message.at[t],
            arrived.at[b, s],
            message_send.at[t],
            message_recv.at[b, s],
            device,
            MESH,
        )

    sends_angles = slab == (to_slab + 1) % slabs

    @pl.when(sends_angles)
    def _():
        for t in range(turns):
            angle_copy(slot, t, (target_of(t), to_slab, cut)).start()

    for ds, dc in offsets:
        trans_copy(cut, slab, ds, dc, (block, (slab + ds) % slabs, (cut + dc) % cuts)).start()
    for side, step in ((0, 1), (1, -1)):

        @pl.when((block + step >= 0) & (block + step < illums))
        def _(side=side, step=step):
            for s, c in everyone:
                edge_copy(side, cut, slab, s, c, (block + step, s, c)).start()

        @pl.when(jnp.logical_not((block - step >= 0) & (block - step < illums)))
        def _(side=side):
            edges[side] = jnp.zeros(edges.shape[1:], jnp.float32)

    for t in range(turns):
        target = target_of(t)
        to_self = (target == block) & loops_back

        @pl.when(jnp.logical_not(to_self))
        def _(t=t, target=target):
            message_copy(slot, slab, t, (target, to_slab, cut)).start()

        @pl.when(to_self)
        def _(t=t):
            arrived[slot, slab] = message[t]

    lead = lane < LANES // 2
    outside = (lead & (block == illums - 1)) | (jnp.logical_not(lead) & (block == 0))
    keep = jnp.where(outside, 0.0, 1.0)
    first_lane, last_lane = lane == 0, lane == LANES - 1

    def laplace(ref, b, slab_id):
        top = PAD + slab_id * rows
        center, vertical, left, right = [], [], [], []
        for tile_id in range(2):
            value = ref[tile_id, b, :, top : top + rows, :]
            center.append(value)
            vertical.append(
                ref[tile_id, b, :, top - 1 : top + rows - 1, :]
                + ref[tile_id, b, :, top + 1 : top + rows + 1, :]
            )
            left.append(pltpu.roll(value, 1, 2))
            right.append(pltpu.roll(value, LANES - 1, 2))
        found = []
        for tile_id in range(2):
            sideways = jnp.where(first_lane, left[1 - tile_id], left[tile_id]) + jnp.where(
                last_lane, right[1 - tile_id], right[tile_id]
            )
            found.append(vertical[tile_id] + sideways - 4.0 * center[tile_id])
        return center, found

    def laplace_pass(ref):
        for b in range(slots):
            for slab_id in range(slabs):
                top = PAD + slab_id * rows
                _, found = laplace(ref, b, slab_id)
                laps[0, b, :, top : top + rows, :] = found[0]
                laps[1, b, :, top : top + rows, :] = found[1] * keep

    def diffracted(ref, b, slab_id, orient):
        top = PAD + slab_id * rows
        once, twice = laplace(laps, b, slab_id)
        result = []
        for tile_id in range(2):
            real = ref[tile_id, b, 0, top : top + rows, :]
            imag = ref[tile_id, b, 1, top : top + rows, :]
            result.append(
                (
                    real
                    - orient * step_coeff * once[tile_id][1]
                    - square_coeff * twice[tile_id][0],
                    imag
                    + orient * step_coeff * once[tile_id][0]
                    - square_coeff * twice[tile_id][1],
                )
            )
        return result

    def pair(tile_id, layer, slab_id):
        ref = trans if tile_id == 0 else trans_edge
        return (
            ref[layer // depth, slab_id, layer % depth, 0],
            ref[layer // depth, slab_id, layer % depth, 1],
        )

    def store(ref, tile_id, b, slab_id, real, imag):
        top = PAD + slab_id * rows
        ref[tile_id, b, 0, top : top + rows, :] = real
        ref[tile_id, b, 1, top : top + rows, :] = imag

    def pass_on(layer, tile_id, b, slab_id, real, imag):
        trans_real, trans_imag = pair(tile_id, layer, slab_id)
        store(
            fields.at[layer],
            tile_id,
            b,
            slab_id,
            trans_real * real - trans_imag * imag,
            trans_real * imag + trans_imag * real,
        )

    for b in range(slots):
        angle_copy(
            b, 0, (source_of(b), (slab + 1) % slabs, cut)
        ).wait_recv()
    starts = {}
    columns = (
        (block * LANES + lane),
        jnp.where(lead, (block + 1) * LANES + lane, (block - 1) * LANES + lane),
    )
    for b in range(slots):
        row_turns = angle_in[b, 0:1, :]
        col_turns = angle_in[b, 4:5, :]
        for tile_id in range(2):
            col_part = col_turns * columns[tile_id].astype(jnp.float32) * (1.0 / total_cols)
            for slab_id in range(slabs):
                row_ids = lax.broadcasted_iota(jnp.int32, (rows, LANES), 0) + slab_id * rows
                row_part = row_turns * row_ids.astype(jnp.float32) * (1.0 / total_rows)
                whole = (col_part - jnp.floor(col_part)) + (row_part - jnp.floor(row_part))
                real, imag = sincos_turns(whole)
                store(fields.at[0], tile_id, b, slab_id, real, imag)

    for ds, dc in offsets:
        trans_copy(
            (cut + cuts - dc) % cuts,
            (slab + slabs - ds) % slabs,
            ds,
            dc,
            (block, (slab + slabs - ds) % slabs, (cut + cuts - dc) % cuts),
        ).wait_recv()
    for side, step in ((0, -1), (1, 1)):

        @pl.when((block + step >= 0) & (block + step < illums))
        def _(side=side, step=step):
            for s, c in everyone:
                edge_copy(side, c, s, s, c, (block + step, s, c)).wait_recv()

    from_right = lane % share < share // 2
    for s, c in everyone:
        both = jnp.where(from_right, edges[1, c, s], edges[0, c, s])
        for q in range(planes):
            trans_edge[c, s, q // 2, q % 2] = (
                both if q == 0 else pltpu.roll(both, LANES - share * q, 1)
            )

    for b in range(slots):
        for tile_id in range(2):
            for slab_id in range(slabs):
                top = PAD + slab_id * rows
                real = fields[0, tile_id, b, 0, top : top + rows, :]
                imag = fields[0, tile_id, b, 1, top : top + rows, :]
                pass_on(0, tile_id, b, slab_id, real, imag)

    adjoint = fields.at[slices]
    for layer in range(slices):
        laplace_pass(fields.at[layer])
        if layer == slices - 1:
            for b in range(slots):
                source = source_of(b)
                for s in range(slabs):

                    @pl.when(jnp.logical_not((source == block) & (slab == s)))
                    def _(b=b, s=s, source=source):
                        message_copy(b, s, 0, (source, s, cut)).wait_recv()

        for b in range(slots):
            for slab_id in range(slabs):
                result = diffracted(fields.at[layer], b, slab_id, 1.0)
                if layer < slices - 1:
                    for tile_id in range(2):
                        pass_on(layer + 1, tile_id, b, slab_id, *result[tile_id])
                else:
                    banded = arrived[b, slab_id, 2 * rows :]
                    rim = jnp.concatenate(
                        [banded]
                        + [pltpu.roll(banded, LANES - 4 * reach * g, 1) for g in range(1, bands)],
                        axis=0,
                    )
                    store(
                        adjoint,
                        0,
                        b,
                        slab_id,
                        result[0][0] - arrived[b, slab_id, :rows],
                        result[0][1] - arrived[b, slab_id, rows : 2 * rows],
                    )
                    store(
                        adjoint,
                        1,
                        b,
                        slab_id,
                        (result[1][0] - rim) * keep,
                        (result[1][1] - pltpu.roll(rim, LANES - 2 * reach, 1)) * keep,
                    )

    def part_copy(layer, slab_id):
        to = layer // depth
        ds = (slab_id + slabs - slab) % slabs
        dc = (to + cuts - cut) % cuts
        return pltpu.make_async_remote_copy(
            parts.at[layer, slab_id],
            others.at[dc, ds, layer % depth],
            part_send.at[layer, slab_id],
            part_recv.at[dc, ds, layer % depth],
            (block, slab_id, to),
            MESH,
        )

    def not_own(layer, slab_id):
        return jnp.logical_not((slab == slab_id) & (cut == layer // depth))

    for layer in reversed(range(slices)):
        laplace_pass(adjoint)
        for slab_id in range(slabs):
            top = PAD + slab_id * rows
            phase_sum, atten_sum = None, None
            for b in range(slots):
                result = diffracted(adjoint, b, slab_id, -1.0)
                real, imag = result[0]
                passed_real = fields[layer, 0, b, 0, top : top + rows, :]
                passed_imag = fields[layer, 0, b, 1, top : top + rows, :]
                phase_part = passed_real * imag - passed_imag * real
                atten_part = -(passed_real * real + passed_imag * imag)
                phase_sum = phase_part if b == 0 else phase_sum + phase_part
                atten_sum = atten_part if b == 0 else atten_sum + atten_part
                if layer > 0:
                    for tile_id in range(2):
                        real, imag = result[tile_id]
                        trans_real, trans_imag = pair(tile_id, layer, slab_id)
                        store(
                            adjoint,
                            tile_id,
                            b,
                            slab_id,
                            trans_real * real + trans_imag * imag,
                            trans_real * imag - trans_imag * real,
                        )
            parts[layer, slab_id, 0] = phase_sum
            parts[layer, slab_id, 1] = atten_sum

            @pl.when(not_own(layer, slab_id))
            def _(layer=layer, slab_id=slab_id):
                part_copy(layer, slab_id).start()

    for k in reversed(range(depth)):
        phase_sum = jnp.zeros((rows, LANES), jnp.float32)
        atten_sum = jnp.zeros((rows, LANES), jnp.float32)
        for ds, dc in offsets:
            pltpu.make_async_remote_copy(
                parts.at[k, 0],
                others.at[dc, ds, k],
                part_send.at[k, 0],
                part_recv.at[dc, ds, k],
                (block, (slab + slabs - ds) % slabs, (cut + cuts - dc) % cuts),
                MESH,
            ).wait_recv()
            phase_sum = phase_sum + others[dc, ds, k, 0]
            atten_sum = atten_sum + others[dc, ds, k, 1]
        out_phase_ref[0, k] = phase_sum
        out_phase_ref[1, k] = atten_sum
        out_atten_ref[0, k] = parts[cut * depth + k, slab, 0]
        out_atten_ref[1, k] = parts[cut * depth + k, slab, 1]

    @pl.when(sends_angles)
    def _():
        for t in range(turns):
            angle_copy(slot, t, (target_of(t), to_slab, cut)).wait_send()

    for ds, dc in offsets:
        trans_copy(cut, slab, ds, dc, (block, (slab + ds) % slabs, (cut + dc) % cuts)).wait_send()
    for side, step in ((0, 1), (1, -1)):

        @pl.when((block + step >= 0) & (block + step < illums))
        def _(side=side, step=step):
            for s, c in everyone:
                edge_copy(side, cut, slab, s, c, (block + step, s, c)).wait_send()

    for t in range(turns):
        target = target_of(t)

        @pl.when(jnp.logical_not((target == block) & loops_back))
        def _(t=t, target=target):
            message_copy(slot, slab, t, (target, to_slab, cut)).wait_send()

    for layer in range(slices):
        for slab_id in range(slabs):

            @pl.when(not_own(layer, slab_id))
            def _(layer=layer, slab_id=slab_id):
                part_copy(layer, slab_id).wait_send()


def fused(phase_delay, attenuation, measured, angles):
    illums, slabs, cuts = (lax.axis_size(name) for name in ("illum", "slab", "cuts"))
    depth, rows, _ = phase_delay.shape
    slots, turns, slices = illums // (slabs * cuts), illums // cuts, depth * cuts
    tall_message = 2 * rows + rows * 8 * slices // LANES
    tall = slabs * rows + 2 * PAD

    def real(*shape):
        return pltpu.VMEM(shape, jnp.float32)

    dma = pltpu.SemaphoreType.DMA
    vmem = pl.BlockSpec(memory_space=pltpu.VMEM)
    own, rest = pl.pallas_call(
        functools.partial(fused_kernel, (illums, slabs, cuts, depth, rows)),
        out_shape=(
            pltpu.VMEM((2,) + phase_delay.shape, jnp.float32),
            pltpu.VMEM((2,) + phase_delay.shape, jnp.float32),
        ),
        in_specs=[pl.BlockSpec(memory_space=pltpu.HBM)] * 4,
        out_specs=(vmem, vmem),
        scratch_shapes=[
            real(cuts, slabs, depth, 2, rows, LANES),
            real(cuts, slabs, depth, 2, rows, LANES),
            real(rows, LANES),
            real(2, cuts, slabs, rows, LANES),
            real(turns, tall_message, LANES),
            real(slots, slabs, tall_message, LANES),
            real(8, LANES),
            real(slots, 8, LANES),
            real(slices + 1, 2, slots, 2, tall, LANES),
            real(2, slots, 2, tall, LANES),
            real(slices, slabs, 2, rows, LANES),
            real(cuts, slabs, depth, 2, rows, LANES),
            real(*phase_delay.shape),
            real(*phase_delay.shape),
            real(*measured.shape),
            pltpu.SMEM(angles.shape, jnp.int32),
            dma((4,)),
            dma((turns,)),
            dma((slots,)),
            dma((slabs, cuts)),
            dma((slabs, cuts)),
            dma((2, cuts, slabs)),
            dma((2, cuts, slabs)),
            dma((turns,)),
            dma((slots, slabs)),
            dma((slices, slabs)),
            dma((cuts, slabs, depth)),
        ],
        compiler_params=pltpu.CompilerParams(
            collective_id=0, has_side_effects=True, vmem_limit_bytes=56 * 1024 * 1024
        ),
    )(phase_delay, attenuation, measured, angles)
    return own[0] + rest[0], own[1] + rest[1]


def solution(mesh):
    placed = (
        P("cuts", "slab", "illum"),
        P("cuts", "slab", "illum"),
        P("illum", None, "slab", None),
        P("illum", None),
    )

    def chosen(*blocks):
        return (fused if suits(*blocks) else body)(*blocks)

    return jax.shard_map(
        chosen,
        mesh=mesh,
        in_specs=placed,
        out_specs=(P("cuts", "slab", "illum"), P("cuts", "slab", "illum")),
        check_vma=False,
    )
```

```python
import functools
import math

import jax
import jax.numpy as jnp
from jax import lax
from jax.experimental import pallas as pl
from jax.experimental.pallas import tpu as pltpu
from jax.sharding import PartitionSpec as P

MESH = pl.DeviceIdType.MESH
LANES = 128
PAD = 8

step_coeff = 0.08
square_coeff = 0.0032


def with_halo(cells, sides, width):
    for axis, dim in sides:
        count = lax.axis_size(axis)
        ends = count - 1
        head = lax.slice_in_dim(cells, 0, width, axis=dim)
        tail = lax.slice_in_dim(cells, cells.shape[dim] - width, cells.shape[dim], axis=dim)
        cells = jnp.concatenate(
            [
                lax.ppermute(tail, axis, [(i, (i + 1) % count) for i in range(ends)]),
                cells,
                lax.ppermute(head, axis, [((i + 1) % count, i) for i in range(ends)]),
            ],
            axis=dim,
        )
    return cells


def shifted(value, axis, steps):
    count = lax.axis_size(axis)
    leading, last = (max(0, -steps), min(count, count - steps))
    return lax.ppermute(value, axis, [(source, source + steps) for source in range(leading, last)])


def lap_rows(padded):
    center = padded[..., 1:-1, :]
    widths = ((0, 0),) * (center.ndim - 1) + ((1, 1),)
    sideways = jnp.pad(center, widths)
    return (
        padded[..., :-2, :]
        + padded[..., 2:, :]
        + sideways[..., :-2]
        + sideways[..., 2:]
        - 4.0 * center
    )


def incident_wave(angles, row_ids, total_rows, total_cols):
    column_ids = jnp.arange(total_cols, dtype=jnp.int32)
    row_turns = angles[:, 0][:, None, None]
    col_turns = angles[:, 1][:, None, None]
    fraction = (
        jnp.mod(row_turns * row_ids[None, :, None], total_rows).astype(jnp.float32) / total_rows
        + jnp.mod(col_turns * column_ids[None, None, :], total_cols).astype(jnp.float32)
        / total_cols
    )
    phase_angle = 2.0 * math.pi * fraction
    return jnp.stack((jnp.cos(phase_angle), jnp.sin(phase_angle)), axis=1)


def complex_times(pair, fields):
    trans_real, trans_imag = pair
    return jnp.stack(
        (
            trans_real * fields[:, 0] - trans_imag * fields[:, 1],
            trans_real * fields[:, 1] + trans_imag * fields[:, 0],
        ),
        axis=1,
    )


def conj_times(pair, fields):
    trans_real, trans_imag = pair
    return jnp.stack(
        (
            trans_real * fields[:, 0] + trans_imag * fields[:, 1],
            trans_real * fields[:, 1] - trans_imag * fields[:, 0],
        ),
        axis=1,
    )


def body(phase_delay, attenuation, measured, angles):
    n_cuts = lax.axis_size("cuts")
    cut_index = lax.axis_index("cuts")
    slab_index = lax.axis_index("slab")
    slab_rows = measured.shape[2]
    n_cols = measured.shape[3]
    total_rows = slab_rows * lax.axis_size("slab")
    row_start = slab_index * slab_rows
    local_phase, local_atten = (phase_delay, attenuation)
    slices_here = local_phase.shape[0]
    row_ids = row_start + jnp.arange(slab_rows, dtype=jnp.int32)
    start_fields = incident_wave(angles, row_ids, total_rows, n_cols)

    def stencil(fields):
        padded = with_halo(fields, (("slab", 2),), 2)
        wide_once = lap_rows(padded)
        wide_ids = row_start + jnp.arange(slab_rows + 2, dtype=jnp.int32) - 1
        inside = (wide_ids >= 0) & (wide_ids < total_rows)
        wide_once = jnp.where(inside[:, None], wide_once, 0.0)
        laplace_one = wide_once[:, :, 1:-1]
        laplace_two = lap_rows(wide_once)
        return (laplace_one, laplace_two)

    def diffract(fields, orient):
        laplace_one, laplace_two = stencil(fields)
        real_part = (
            fields[:, 0]
            - orient * step_coeff * laplace_one[:, 1]
            - square_coeff * laplace_two[:, 0]
        )
        imag_part = (
            fields[:, 1]
            + orient * step_coeff * laplace_one[:, 0]
            - square_coeff * laplace_two[:, 1]
        )
        return jnp.stack((real_part, imag_part), axis=1)

    whole_phase, whole_atten = (
        lax.all_gather(local_phase, "illum", axis=2, tiled=True),
        lax.all_gather(local_atten, "illum", axis=2, tiled=True),
    )
    transmit = []
    for layer_index in range(slices_here):
        damping = jnp.exp(-whole_atten[layer_index])
        transmit.append(
            (
                damping * jnp.cos(whole_phase[layer_index]),
                damping * jnp.sin(whole_phase[layer_index]),
            )
        )
    phase_list = [None] * slices_here
    atten_list = [None] * slices_here

    def record(layer_index, passed, weighted):
        phase_part = -jnp.sum(passed[:, 1] * weighted[:, 0] - passed[:, 0] * weighted[:, 1], axis=0)
        atten_part = -jnp.sum(passed[:, 0] * weighted[:, 0] + passed[:, 1] * weighted[:, 1], axis=0)
        phase_list[layer_index] = phase_part
        atten_list[layer_index] = atten_part

    entering = start_fields
    stored = []
    fields = start_fields
    for round_index in range(n_cuts):
        fields = entering
        stored = []
        for layer_index in range(slices_here):
            passed = complex_times(transmit[layer_index], fields)
            stored.append(passed)
            fields = diffract(passed, 1.0)
        if round_index < n_cuts - 1:
            received = shifted(fields, "cuts", 1)
            entering = jnp.where(cut_index == 0, start_fields, received)
    residual = fields - measured
    entering = residual
    for round_index in range(n_cuts):
        adjoint = entering
        last_round = round_index == n_cuts - 1
        for layer_index in reversed(range(slices_here)):
            weighted = diffract(adjoint, -1.0)
            if last_round:
                record(layer_index, stored[layer_index], weighted)
            adjoint = conj_times(transmit[layer_index], weighted)
        if not last_round:
            received = shifted(adjoint, "cuts", -1)
            entering = jnp.where(cut_index == n_cuts - 1, residual, received)
    grad_phase, grad_atten = (
        lax.psum_scatter(jnp.stack(phase_list), "illum", scatter_dimension=2, tiled=True),
        lax.psum_scatter(jnp.stack(atten_list), "illum", scatter_dimension=2, tiled=True),
    )
    return (grad_phase, grad_atten)


def suits(phase_delay, attenuation, measured, angles):
    illums, slabs, cuts = (lax.axis_size(name) for name in ("illum", "slab", "cuts"))
    depth, rows, width = phase_delay.shape
    halo = 4 * depth * cuts
    return (
        width == LANES
        and rows % 8 == 0
        and measured.shape[0] == 1
        and measured.shape[3] == illums * LANES
        and illums % (slabs * cuts) == 0
        and illums % (2 * cuts) == 0
        and rows % 32 == 0
        and LANES % (8 * depth * cuts) == 0
        and slabs > 1
        and illums // (slabs * cuts) <= 4
        and slabs * rows <= 128
        and LANES % (2 * depth) == 0
        and 2 * depth * 2 * halo <= LANES
    )


def sincos_turns(turns):
    quarter = jnp.round(4.0 * turns)
    angle = (turns - 0.25 * quarter) * (2.0 * math.pi)
    square = angle * angle
    sine = angle * (
        1.0 + square * (-1.0 / 6 + square * (1.0 / 120 + square * (-1.0 / 5040 + square / 362880)))
    )
    cosine = 1.0 + square * (
        -0.5 + square * (1.0 / 24 + square * (-1.0 / 720 + square / 40320))
    )
    place = quarter - 4.0 * jnp.floor(0.25 * quarter)
    odd = (place == 1.0) | (place == 3.0)
    first = jnp.where(odd, sine, cosine)
    second = jnp.where(odd, cosine, sine)
    cos_value = jnp.where((place == 1.0) | (place == 2.0), -first, first)
    sin_value = jnp.where(place >= 2.0, -second, second)
    return cos_value, sin_value


def fused_kernel(
    sizes,
    phase_hbm,
    atten_hbm,
    measured_hbm,
    angles_hbm,
    out_phase_ref,
    out_atten_ref,
    trans,
    trans_edge,
    edge_own,
    edges,
    message,
    arrived,
    angle_own,
    angle_in,
    fields,
    laps,
    parts,
    others,
    phase_ref,
    atten_ref,
    measured_ref,
    angles_ref,
    load_sem,
    angle_send,
    angle_recv,
    trans_send,
    trans_recv,
    edge_send,
    edge_recv,
    message_send,
    message_recv,
    part_send,
    part_recv,
):
    illums, slabs, cuts, depth, rows = sizes
    members = slabs * cuts
    slots = illums // members
    reach = 2 * depth * cuts
    bands = LANES // (4 * reach)
    band = rows // bands
    turns = illums // cuts
    slices = depth * cuts
    total_rows = slabs * rows
    total_cols = illums * LANES
    planes = 2 * depth
    share = LANES // planes

    block = lax.axis_index("illum")
    slab = lax.axis_index("slab")
    cut = lax.axis_index("cuts")
    own_pair, own_side = block // 2, block % 2
    entry = own_side + 2 * (own_pair // cuts)
    to_slab, slot = entry % slabs, entry // slabs
    phase_of_cut = (cut + cuts - own_pair % cuts) % cuts

    def target_of(t):
        return 2 * (cuts * (t // 2) + phase_of_cut) + t % 2

    def source_of(b):
        e = slab + slabs * b
        return 2 * (cuts * (e // 2) + phase_of_cut) + e % 2

    loads = [
        pltpu.make_async_copy(angles_hbm, angles_ref, load_sem.at[0]),
        pltpu.make_async_copy(phase_hbm, phase_ref, load_sem.at[1]),
        pltpu.make_async_copy(atten_hbm, atten_ref, load_sem.at[2]),
        pltpu.make_async_copy(measured_hbm, measured_ref, load_sem.at[3]),
    ]
    for load in loads:
        load.start()
    offsets = [(ds, dc) for ds in range(slabs) for dc in range(cuts) if ds + dc > 0]
    everyone = [(s, c) for s in range(slabs) for c in range(cuts)]
    loops_back = (phase_of_cut == own_pair % cuts) & (to_slab == slab)

    barrier = pltpu.get_barrier_semaphore()

    def greet(device):
        pl.semaphore_signal(barrier, inc=1, device_id=device, device_id_type=MESH)

    for b in range(slots):
        for s in range(slabs):
            source = source_of(b)

            @pl.when(jnp.logical_not((source == block) & (slab == s)))
            def _(source=source, s=s):
                greet((source, s, cut))

    for step in (-1, 1):

        @pl.when((block + step >= 0) & (block + step < illums))
        def _(step=step):
            for s, c in everyone:
                greet((block + step, s, c))

    for ds, dc in offsets:
        greet((block, (slab + ds) % slabs, (cut + dc) % cuts))

    lane = lax.broadcasted_iota(jnp.int32, (1, LANES), 1)

    loads[1].wait()
    loads[2].wait()
    packed = None
    for k in range(depth):
        damping = jnp.exp(-atten_ref[k])
        cosine, sine = sincos_turns(phase_ref[k] * (0.5 / math.pi))
        for part, value in ((0, damping * cosine), (1, damping * sine)):
            trans[cut, slab, k, part] = value
            q = 2 * k + part
            if q == 0:
                packed = value
            else:
                here = (lane >= share * q - share // 2) & (lane < share * q + share // 2)
                packed = jnp.where(here, pltpu.roll(value, share * q, 1), packed)
    edge_own[...] = packed
    loads[0].wait()
    angle_rows = lax.broadcasted_iota(jnp.int32, (8, LANES), 0)
    angle_own[...] = jnp.where(angle_rows < 4, angles_ref[0, 0], angles_ref[0, 1]).astype(
        jnp.float32
    )

    loads[3].wait()
    for t in range(turns):
        target = target_of(t)
        before, after = jnp.maximum(target - 1, 0), jnp.minimum(target + 1, illums - 1)

        def tile(part, at):
            return measured_ref[0, part, :, pl.ds(pl.multiple_of(at * LANES, LANES), LANES)]

        rims = []
        for part in range(2):
            message[t, part * rows : (part + 1) * rows] = tile(part, target)
            rims.append(jnp.where(lane < LANES // 2, tile(part, after), tile(part, before)))
        second = (lane >= reach) & (lane < 3 * reach)
        rim = jnp.where(second, pltpu.roll(rims[1], 2 * reach, 1), rims[0])
        packed = rim[:band]
        for g in range(1, bands):
            here = ((lane + reach) // (4 * reach)) % bands == g
            moved = pltpu.roll(rim[g * band : (g + 1) * band], 4 * reach * g, 1)
            packed = jnp.where(here, moved, packed)
        message[t, 2 * rows :] = packed

    for ref in (fields, laps):
        zero = jnp.zeros(ref.shape[:-2] + (PAD, LANES), jnp.float32)
        ref[..., 0:PAD, :] = zero
        ref[..., PAD + total_rows : 2 * PAD + total_rows, :] = zero

    inside_low = (block > 0).astype(jnp.int32)
    inside_high = (block < illums - 1).astype(jnp.int32)
    pl.semaphore_wait(
        barrier,
        len(offsets) + members * (inside_low + inside_high) + turns - loops_back.astype(jnp.int32),
    )

    def angle_copy(b, t, device):
        return pltpu.make_async_remote_copy(
            angle_own, angle_in.at[b], angle_send.at[t], angle_recv.at[b], device, MESH
        )

    def trans_copy(c, s, ds, dc, device):
        return pltpu.make_async_remote_copy(
            trans.at[c, s],
            trans.at[c, s],
            trans_send.at[ds, dc],
            trans_recv.at[ds, dc],
            device,
            MESH,
        )

    def edge_copy(side, c, s, to_s, to_c, device):
        return pltpu.make_async_remote_copy(
            edge_own,
            edges.at[side, c, s],
            edge_send.at[side, to_c, to_s],
            edge_recv.at[side, c, s],
            device,
            MESH,
        )

    def message_copy(b, s, t, device):
        return pltpu.make_async_remote_copy(
            message.at[t],
            arrived.at[b, s],
            message_send.at[t],
            message_recv.at[b, s],
            device,
            MESH,
        )

    sends_angles = slab == (to_slab + 1) % slabs

    @pl.when(sends_angles)
    def _():
        for t in range(turns):
            angle_copy(slot, t, (target_of(t), to_slab, cut)).start()

    for ds, dc in offsets:
        trans_copy(cut, slab, ds, dc, (block, (slab + ds) % slabs, (cut + dc) % cuts)).start()
    for side, step in ((0, 1), (1, -1)):

        @pl.when((block + step >= 0) & (block + step < illums))
        def _(side=side, step=step):
            for s, c in everyone:
                edge_copy(side, cut, slab, s, c, (block + step, s, c)).start()

        @pl.when(jnp.logical_not((block - step >= 0) & (block - step < illums)))
        def _(side=side):
            edges[side] = jnp.zeros(edges.shape[1:], jnp.float32)

    for t in range(turns):
        target = target_of(t)
        to_self = (target == block) & loops_back

        @pl.when(jnp.logical_not(to_self))
        def _(t=t, target=target):
            message_copy(slot, slab, t, (target, to_slab, cut)).start()

        @pl.when(to_self)
        def _(t=t):
            arrived[slot, slab] = message[t]

    lead = lane < LANES // 2
    outside = (lead & (block == illums - 1)) | (jnp.logical_not(lead) & (block == 0))
    keep = jnp.where(outside, 0.0, 1.0)
    first_lane, last_lane = lane == 0, lane == LANES - 1

    def laplace(ref, b, slab_id):
        top = PAD + slab_id * rows
        center, vertical, left, right = [], [], [], []
        for tile_id in range(2):
            value = ref[tile_id, b, :, top : top + rows, :]
            center.append(value)
            vertical.append(
                ref[tile_id, b, :, top - 1 : top + rows - 1, :]
                + ref[tile_id, b, :, top + 1 : top + rows + 1, :]
            )
            left.append(pltpu.roll(value, 1, 2))
            right.append(pltpu.roll(value, LANES - 1, 2))
        found = []
        for tile_id in range(2):
            sideways = jnp.where(first_lane, left[1 - tile_id], left[tile_id]) + jnp.where(
                last_lane, right[1 - tile_id], right[tile_id]
            )
            found.append(vertical[tile_id] + sideways - 4.0 * center[tile_id])
        return center, found

    def laplace_pass(ref):
        for b in range(slots):
            for slab_id in range(slabs):
                top = PAD + slab_id * rows
                _, found = laplace(ref, b, slab_id)
                laps[0, b, :, top : top + rows, :] = found[0]
                laps[1, b, :, top : top + rows, :] = found[1] * keep

    def diffracted(ref, b, slab_id, orient):
        top = PAD + slab_id * rows
        once, twice = laplace(laps, b, slab_id)
        result = []
        for tile_id in range(2):
            real = ref[tile_id, b, 0, top : top + rows, :]
            imag = ref[tile_id, b, 1, top : top + rows, :]
            result.append(
                (
                    real
                    - orient * step_coeff * once[tile_id][1]
                    - square_coeff * twice[tile_id][0],
                    imag
                    + orient * step_coeff * once[tile_id][0]
                    - square_coeff * twice[tile_id][1],
                )
            )
        return result

    def pair(tile_id, layer, slab_id):
        ref = trans if tile_id == 0 else trans_edge
        return (
            ref[layer // depth, slab_id, layer % depth, 0],
            ref[layer // depth, slab_id, layer % depth, 1],
        )

    def store(ref, tile_id, b, slab_id, real, imag):
        top = PAD + slab_id * rows
        ref[tile_id, b, 0, top : top + rows, :] = real
        ref[tile_id, b, 1, top : top + rows, :] = imag

    def pass_on(layer, tile_id, b, slab_id, real, imag):
        trans_real, trans_imag = pair(tile_id, layer, slab_id)
        store(
            fields.at[layer],
            tile_id,
            b,
            slab_id,
            trans_real * real - trans_imag * imag,
            trans_real * imag + trans_imag * real,
        )

    for b in range(slots):
        angle_copy(
            b, 0, (source_of(b), (slab + 1) % slabs, cut)
        ).wait_recv()
    starts = {}
    columns = (
        (block * LANES + lane),
        jnp.where(lead, (block + 1) * LANES + lane, (block - 1) * LANES + lane),
    )
    for b in range(slots):
        row_turns = angle_in[b, 0:1, :]
        col_turns = angle_in[b, 4:5, :]
        for tile_id in range(2):
            col_part = col_turns * columns[tile_id].astype(jnp.float32) * (1.0 / total_cols)
            for slab_id in range(slabs):
                row_ids = lax.broadcasted_iota(jnp.int32, (rows, LANES), 0) + slab_id * rows
                row_part = row_turns * row_ids.astype(jnp.float32) * (1.0 / total_rows)
                whole = (col_part - jnp.floor(col_part)) + (row_part - jnp.floor(row_part))
                real, imag = sincos_turns(whole)
                store(fields.at[0], tile_id, b, slab_id, real, imag)

    for ds, dc in offsets:
        trans_copy(
            (cut + cuts - dc) % cuts,
            (slab + slabs - ds) % slabs,
            ds,
            dc,
            (block, (slab + slabs - ds) % slabs, (cut + cuts - dc) % cuts),
        ).wait_recv()
    for side, step in ((0, -1), (1, 1)):

        @pl.when((block + step >= 0) & (block + step < illums))
        def _(side=side, step=step):
            for s, c in everyone:
                edge_copy(side, c, s, s, c, (block + step, s, c)).wait_recv()

    from_right = lane % share < share // 2
    for s, c in everyone:
        both = jnp.where(from_right, edges[1, c, s], edges[0, c, s])
        for q in range(planes):
            trans_edge[c, s, q // 2, q % 2] = (
                both if q == 0 else pltpu.roll(both, LANES - share * q, 1)
            )

    for b in range(slots):
        for tile_id in range(2):
            for slab_id in range(slabs):
                top = PAD + slab_id * rows
                real = fields[0, tile_id, b, 0, top : top + rows, :]
                imag = fields[0, tile_id, b, 1, top : top + rows, :]
                pass_on(0, tile_id, b, slab_id, real, imag)

    adjoint = fields.at[slices]
    for layer in range(slices):
        laplace_pass(fields.at[layer])
        if layer == slices - 1:
            for b in range(slots):
                source = source_of(b)
                for s in range(slabs):

                    @pl.when(jnp.logical_not((source == block) & (slab == s)))
                    def _(b=b, s=s, source=source):
                        message_copy(b, s, 0, (source, s, cut)).wait_recv()

        for b in range(slots):
            for slab_id in range(slabs):
                result = diffracted(fields.at[layer], b, slab_id, 1.0)
                if layer < slices - 1:
                    for tile_id in range(2):
                        pass_on(layer + 1, tile_id, b, slab_id, *result[tile_id])
                else:
                    banded = arrived[b, slab_id, 2 * rows :]
                    rim = jnp.concatenate(
                        [banded]
                        + [pltpu.roll(banded, LANES - 4 * reach * g, 1) for g in range(1, bands)],
                        axis=0,
                    )
                    store(
                        adjoint,
                        0,
                        b,
                        slab_id,
                        result[0][0] - arrived[b, slab_id, :rows],
                        result[0][1] - arrived[b, slab_id, rows : 2 * rows],
                    )
                    store(
                        adjoint,
                        1,
                        b,
                        slab_id,
                        (result[1][0] - rim) * keep,
                        (result[1][1] - pltpu.roll(rim, LANES - 2 * reach, 1)) * keep,
                    )

    def part_copy(layer, slab_id):
        to = layer // depth
        ds = (slab_id + slabs - slab) % slabs
        dc = (to + cuts - cut) % cuts
        return pltpu.make_async_remote_copy(
            parts.at[layer, slab_id],
            others.at[dc, ds, layer % depth],
            part_send.at[layer, slab_id],
            part_recv.at[dc, ds, layer % depth],
            (block, slab_id, to),
            MESH,
        )

    def not_own(layer, slab_id):
        return jnp.logical_not((slab == slab_id) & (cut == layer // depth))

    for layer in reversed(range(slices)):
        laplace_pass(adjoint)
        for slab_id in range(slabs):
            top = PAD + slab_id * rows
            phase_sum, atten_sum = None, None
            for b in range(slots):
                result = diffracted(adjoint, b, slab_id, -1.0)
                real, imag = result[0]
                passed_real = fields[layer, 0, b, 0, top : top + rows, :]
                passed_imag = fields[layer, 0, b, 1, top : top + rows, :]
                phase_part = passed_real * imag - passed_imag * real
                atten_part = -(passed_real * real + passed_imag * imag)
                phase_sum = phase_part if b == 0 else phase_sum + phase_part
                atten_sum = atten_part if b == 0 else atten_sum + atten_part
                if layer > 0:
                    for tile_id in range(2):
                        real, imag = result[tile_id]
                        trans_real, trans_imag = pair(tile_id, layer, slab_id)
                        store(
                            adjoint,
                            tile_id,
                            b,
                            slab_id,
                            trans_real * real + trans_imag * imag,
                            trans_real * imag - trans_imag * real,
                        )
            parts[layer, slab_id, 0] = phase_sum
            parts[layer, slab_id, 1] = atten_sum

            @pl.when(not_own(layer, slab_id))
            def _(layer=layer, slab_id=slab_id):
                part_copy(layer, slab_id).start()

    for k in reversed(range(depth)):
        phase_sum = jnp.zeros((rows, LANES), jnp.float32)
        atten_sum = jnp.zeros((rows, LANES), jnp.float32)
        for ds, dc in offsets:
            pltpu.make_async_remote_copy(
                parts.at[k, 0],
                others.at[dc, ds, k],
                part_send.at[k, 0],
                part_recv.at[dc, ds, k],
                (block, (slab + slabs - ds) % slabs, (cut + cuts - dc) % cuts),
                MESH,
            ).wait_recv()
            phase_sum = phase_sum + others[dc, ds, k, 0]
            atten_sum = atten_sum + others[dc, ds, k, 1]
        out_phase_ref[0, k] = phase_sum
        out_phase_ref[1, k] = atten_sum
        out_atten_ref[0, k] = parts[cut * depth + k, slab, 0]
        out_atten_ref[1, k] = parts[cut * depth + k, slab, 1]

    @pl.when(sends_angles)
    def _():
        for t in range(turns):
            angle_copy(slot, t, (target_of(t), to_slab, cut)).wait_send()

    for ds, dc in offsets:
        trans_copy(cut, slab, ds, dc, (block, (slab + ds) % slabs, (cut + dc) % cuts)).wait_send()
    for side, step in ((0, 1), (1, -1)):

        @pl.when((block + step >= 0) & (block + step < illums))
        def _(side=side, step=step):
            for s, c in everyone:
                edge_copy(side, cut, slab, s, c, (block + step, s, c)).wait_send()

    for t in range(turns):
        target = target_of(t)

        @pl.when(jnp.logical_not((target == block) & loops_back))
        def _(t=t, target=target):
            message_copy(slot, slab, t, (target, to_slab, cut)).wait_send()

    for layer in range(slices):
        for slab_id in range(slabs):

            @pl.when(not_own(layer, slab_id))
            def _(layer=layer, slab_id=slab_id):
                part_copy(layer, slab_id).wait_send()


def fused(phase_delay, attenuation, measured, angles):
    illums, slabs, cuts = (lax.axis_size(name) for name in ("illum", "slab", "cuts"))
    depth, rows, _ = phase_delay.shape
    slots, turns, slices = illums // (slabs * cuts), illums // cuts, depth * cuts
    tall_message = 2 * rows + rows * 8 * slices // LANES
    tall = slabs * rows + 2 * PAD

    def real(*shape):
        return pltpu.VMEM(shape, jnp.float32)

    dma = pltpu.SemaphoreType.DMA
    vmem = pl.BlockSpec(memory_space=pltpu.VMEM)
    own, rest = pl.pallas_call(
        functools.partial(fused_kernel, (illums, slabs, cuts, depth, rows)),
        out_shape=(
            pltpu.VMEM((2,) + phase_delay.shape, jnp.float32),
            pltpu.VMEM((2,) + phase_delay.shape, jnp.float32),
        ),
        in_specs=[pl.BlockSpec(memory_space=pltpu.HBM)] * 4,
        out_specs=(vmem, vmem),
        scratch_shapes=[
            real(cuts, slabs, depth, 2, rows, LANES),
            real(cuts, slabs, depth, 2, rows, LANES),
            real(rows, LANES),
            real(2, cuts, slabs, rows, LANES),
            real(turns, tall_message, LANES),
            real(slots, slabs, tall_message, LANES),
            real(8, LANES),
            real(slots, 8, LANES),
            real(slices + 1, 2, slots, 2, tall, LANES),
            real(2, slots, 2, tall, LANES),
            real(slices, slabs, 2, rows, LANES),
            real(cuts, slabs, depth, 2, rows, LANES),
            real(*phase_delay.shape),
            real(*phase_delay.shape),
            real(*measured.shape),
            pltpu.SMEM(angles.shape, jnp.int32),
            dma((4,)),
            dma((turns,)),
            dma((slots,)),
            dma((slabs, cuts)),
            dma((slabs, cuts)),
            dma((2, cuts, slabs)),
            dma((2, cuts, slabs)),
            dma((turns,)),
            dma((slots, slabs)),
            dma((slices, slabs)),
            dma((cuts, slabs, depth)),
        ],
        compiler_params=pltpu.CompilerParams(
            collective_id=0, has_side_effects=True, vmem_limit_bytes=56 * 1024 * 1024
        ),
    )(phase_delay, attenuation, measured, angles)
    return own[0] + rest[0], own[1] + rest[1]


def solution(mesh):
    placed = (
        P("cuts", "slab", "illum"),
        P("cuts", "slab", "illum"),
        P("illum", None, "slab", None),
        P("illum", None),
    )

    def chosen(*blocks):
        return (fused if suits(*blocks) else body)(*blocks)

    return jax.shard_map(
        chosen,
        mesh=mesh,
        in_specs=placed,
        out_specs=(P("cuts", "slab", "illum"), P("cuts", "slab", "illum")),
        check_vma=False,
    )
```
